512 devices in a mesh: dp: 4 (over y), pipe: 16 (over z), tensor: 8 (over x, core).
Axes of the slice: x: 4, y: 4, z: 16, core: 2. Of those that a mesh axis runs over, the one named last changes fastest.
Arguments:
- hidden: bfloat16 [512, 8192], P('dp', ('pipe', 'tensor')), parts along dimension 0
- weight: bfloat16 [65536, 8192], P(('dp', 'pipe', 'tensor')), parts along dimension 0
- targets: int32 [512], P('dp'), parts along dimension 0, may hold values from 0 to 16383
Outputs:
- d_hidden: bfloat16 [512, 8192], P('dp', ('pipe', 'tensor')), parts along dimension 0
- d_weight: bfloat16 [65536, 8192], P(('dp', 'pipe', 'tensor')), parts along dimension 0
- losses: float32 [512], P('dp'), parts along dimension 0
The draws below stay inside these ranges and needn't reach their ends.
There are 4 independent parts, one for each index of `dp`. The reference program is written for one: setup_inputs(seed, part) draws one part's arguments, and reference() takes and returns one part's arrays. A program takes and returns all parts, laid end to end along the dimension named above; each array names one. Nothing has to cross between parts.
All inputs are finite; a program needn't handle non-finite values.
Results may differ from the reference program's by a relative error of at most 0.0034.
Values may be sent and summed in bfloat16 or wider, within the bound.
A program may use at most 64 MiB of HBM per device.

```python
import math
import jax
import jax.numpy as jnp
from jax import lax

D = 8192
TOKENS = 128
VOCAB = 16384


def weight_base(key):
    return jax.random.normal(key, (VOCAB, D), jnp.float32) * (3.0 / math.sqrt(D))


def draw_weight(key, part):
    base = weight_base(key)
    return base.astype(jnp.bfloat16)


def draw_hidden(key, part):
    key = jax.random.fold_in(key, 23)
    first_key = jax.random.fold_in(key, 0)
    rows = jax.random.normal(first_key, (TOKENS, D), jnp.float32)
    return rows.astype(jnp.bfloat16)


def with_ends(result, rng, smallest, high):
    longest = result.shape.index(max(result.shape))
    spots = []
    for shift in (0, 1):
        where = [jax.random.randint(jax.random.fold_in(rng, axis), (), 0, length) for axis, length in enumerate(result.shape)]
        where[longest] = (where[longest] + shift) % result.shape[longest]
        spots.append(tuple(where))
    return result.at[spots[0]].set(smallest).at[spots[1]].set(high)


def setup_inputs(seed: int = 0, part: int = 0) -> dict:
    key_list = jax.random.split(jax.random.key(seed), 4)
    own_keys = jax.random.split(jax.random.fold_in(key_list[3], part), 4)
    hidden = draw_hidden(jax.random.fold_in(jax.random.fold_in(key_list[3], part), 71), part)
    weight = draw_weight(jax.random.fold_in(jax.random.fold_in(key_list[3], part), 71), part)
    targets = with_ends(jax.random.randint(own_keys[2], (TOKENS,), 0, VOCAB), jax.random.fold_in(own_keys[2], 1), 0, VOCAB - 1).astype(jnp.int32)
    return dict(hidden=hidden, weight=weight, targets=targets)


def reference(hidden, weight, targets):
    logits = lax.dot_general(hidden, weight, (((1,), (1,)), ((), ())), preferred_element_type=jnp.float32)
    row_top = jnp.max(logits, axis=1)
    exponent = jnp.exp(logits - row_top[:, None])
    row_total = jnp.sum(exponent, axis=1)
    row_pick = jnp.take_along_axis(logits, targets[:, None].astype(jnp.int32), axis=1)[:, 0]
    losses = row_top + jnp.log(row_total) - row_pick
    column = lax.broadcasted_iota(jnp.int32, logits.shape, 1)
    is_target = (column == targets[:, None]).astype(jnp.float32)
    grad_logits = (exponent / row_total[:, None] - is_target).astype(jnp.bfloat16)
    d_hidden = jnp.dot(grad_logits, weight, preferred_element_type=jnp.float32).astype(jnp.bfloat16)
    d_weight = lax.dot_general(grad_logits, hidden, (((0,), (0,)), ((), ())), preferred_element_type=jnp.float32).astype(jnp.bfloat16)
    return d_hidden, d_weight, losses
```

```python
import functools

import jax
import jax.numpy as jnp
from jax import lax
from jax.experimental import pallas as pl
from jax.experimental.pallas import tpu as pltpu
from jax.sharding import PartitionSpec as P

MESH = pl.DeviceIdType.MESH
NZ, NX, NT = 16, 4, 8
NEAR = (1, -1, 2, -2)
OFFSETS = [0, 5, -5, 8] + [b + a for b in NEAR for a in (0, 5, -5)]
GROUPS = [(0, 4), (4, 6), (10, 6)]
MESSAGES = 96


def kernel(hidden_hbm, weight_hbm, targets_ref, d_hidden_ref, d_weight_hbm, losses_ref,
           own, w, wsend, wx, packed, full, logits_x, stat_t, stat_z, stat_own, stat_mid,
           product, pieces, near_sum, far_sum, opposite, d_w, local_sem, send, recv):
    dp, z, t = lax.axis_index("dp"), lax.axis_index("pipe"), lax.axis_index("tensor")
    x, c = t // 2, lax.rem(t, 2)
    partner = (dp, z, 2 * x + 1 - c)

    def at_z(offset):
        return (dp, lax.rem(z + offset + NZ, NZ), t)

    def at_t(k):
        return (dp, z, lax.rem(t + k, NT))

    def x_at(k):
        return lax.rem(x + k + NX, NX)

    load_h = pltpu.make_async_copy(hidden_hbm, own, local_sem.at[0])
    load_w = pltpu.make_async_copy(weight_hbm, w, local_sem.at[1])
    load_h.start()
    load_w.start()
    barrier = pltpu.get_barrier_semaphore()
    for k in range(1, NZ):
        pl.semaphore_signal(barrier, inc=1, device_id=at_z(k), device_id_type=MESH)
    for k in range(1, NT):
        pl.semaphore_signal(barrier, inc=1, device_id=at_t(k), device_id_type=MESH)

    count = [0]
    sent = []

    def new():
        count[0] += 1
        return count[0] - 1

    def push(src, dst, k, device):
        copy = pltpu.make_async_remote_copy(
            src, dst, send.at[k], recv.at[k], device_id=device, device_id_type=MESH)
        copy.start()
        sent.append(copy)

    def landed(ref, k):
        pltpu.make_async_remote_copy(
            ref, ref, send.at[k], recv.at[k], device_id=partner, device_id_type=MESH).wait_recv()

    load_h.wait()
    packed[t, 0] = jnp.concatenate([own[0:64, :], own[64:128, :]], axis=1)
    load_w.wait()
    for xx in range(NX):
        for j in range(NZ // 2):
            first = w[:, (8 * j + xx) * 128:(8 * j + xx + 1) * 128]
            second = w[:, (8 * j + 4 + xx) * 128:(8 * j + 5 + xx) * 128]
            wsend[2 * xx, :, j * 128:(j + 1) * 128] = jnp.concatenate(
                [first[:, :64], second[:, :64]], axis=1)
            wsend[2 * xx + 1, :, j * 128:(j + 1) * 128] = jnp.concatenate(
                [first[:, 64:], second[:, 64:]], axis=1)
    pl.semaphore_wait(barrier, NZ - 1 + NT - 1)

    level1 = {}
    for slot, offset in ((1, 5), (2, -5), (3, 8)):
        level1[slot] = new()
        push(packed.at[t, 0], packed.at[t, slot], level1[slot], at_z(-offset))
    w_message = [None] + [new() for _ in range(NT - 1)]

    def push_w(k):
        there = lax.rem(t + k, NT)
        push(wsend.at[there], wx.at[t], w_message[k], at_t(k))

    for k in (1, 7, 2, 6):
        push_w(k)

    landed(packed.at[t, 1], level1[1])
    landed(packed.at[t, 2], level1[2])
    level2 = []
    for i, b in enumerate(NEAR):
        level2.append(new())
        push(packed.at[t, pl.ds(0, 3)], packed.at[t, pl.ds(4 + 3 * i, 3)], level2[i], at_z(-b))
    landed(packed.at[t, 3], level1[3])

    x_message = [[None] + [new() for _ in range(NX - 1)] for _ in GROUPS]
    core_message = [[new() for _ in range(NX)] for _ in GROUPS]

    def push_x(g):
        start, size = GROUPS[g]
        part = packed.at[t, pl.ds(start, size)]
        for k in (2, 1, 3):
            push(part, part, x_message[g][k], (dp, z, 2 * x_at(k) + c))
        push(part, part, core_message[g][0], partner)

    def pass_on(g):
        start, size = GROUPS[g]
        for k in (1, 3, 2):
            part = packed.at[2 * x_at(-k) + c, pl.ds(start, size)]
            landed(part, x_message[g][k])
            push(part, part, core_message[g][k], partner)

    column_half = lax.broadcasted_iota(jnp.int32, (64, 128), 1) < 64
    total = [jnp.zeros((128, 128), jnp.float32)]

    def absorb(g):
        start, size = GROUPS[g]
        for k in range(NX):
            landed(packed.at[2 * x_at(-k) + 1 - c, pl.ds(start, size)], core_message[g][k])
        for slot in range(start, start + size):
            there = lax.rem(z + OFFSETS[slot] + NZ, NZ)
            rows = []
            for xx in range(NX):
                even, odd = packed[2 * xx, slot], packed[2 * xx + 1, slot]
                low = jnp.concatenate([even[:, :64], odd[:, :64]], axis=1)
                high = jnp.concatenate([even[:, 64:], odd[:, 64:]], axis=1)
                rows.append(jnp.concatenate([low, high], axis=0))
            block = jnp.concatenate(rows, axis=1)
            columns = pl.ds(pl.multiple_of(there * 512, 512), 512)
            full[:, columns] = block
            total[0] = total[0] + lax.dot_general(
                w[:, columns], block, (((1,), (1,)), ((), ())),
                preferred_element_type=jnp.float32)

    push_x(0)
    landed(packed.at[t, pl.ds(4, 3)], level2[0])
    landed(packed.at[t, pl.ds(7, 3)], level2[1])
    push_x(1)
    landed(packed.at[t, pl.ds(10, 3)], level2[2])
    landed(packed.at[t, pl.ds(13, 3)], level2[3])
    push_x(2)
    for k in (3, 5, 4):
        push_w(k)
    pass_on(0)
    absorb(0)
    pass_on(1)
    pass_on(2)
    absorb(1)
    absorb(2)

    logits = total[0]
    first_row = (z * NT + t) * 128
    row = lax.broadcasted_iota(jnp.int32, (128, 128), 0)
    target = targets_ref[...]
    is_target = (row + first_row) == target
    top = jnp.max(logits, axis=0, keepdims=True)
    stat_own[:, 0:128] = top
    stat_own[:, 128:256] = jnp.sum(jnp.exp(logits - top), axis=0, keepdims=True)
    stat_own[:, 256:384] = jnp.sum(jnp.where(is_target, logits, 0.0), axis=0, keepdims=True)
    stat_t[0] = stat_own[...]
    stat_t_message = [None] + [new() for _ in range(NT - 1)]
    for k in range(1, NT):
        push(stat_own, stat_t.at[k], stat_t_message[k], at_t(k))
    logits_x[t] = logits.T
    logits_message = [None] + [new() for _ in range(NT - 1)]
    for k in range(1, NT):
        push(logits_x.at[t], logits_x.at[t], logits_message[k], at_t(k))

    def combine(stats, n):
        top = stats[0, :, 0:128]
        for k in range(1, n):
            top = jnp.maximum(top, stats[k, :, 0:128])
        total = jnp.zeros_like(top)
        pick = jnp.zeros_like(top)
        for k in range(n):
            total = total + stats[k, :, 128:256] * jnp.exp(stats[k, :, 0:128] - top)
            pick = pick + stats[k, :, 256:384]
        return top, total, pick

    for k in range(1, NT):
        landed(stat_t.at[k], stat_t_message[k])
    top, row_total, pick = combine(stat_t, NT)
    stat_mid[:, 0:128] = top
    stat_mid[:, 128:256] = row_total
    stat_mid[:, 256:384] = pick
    stat_z[0] = stat_mid[...]
    stat_z_message = [None] + [new() for _ in range(NZ - 1)]
    for k in (8, 7, 9, 6, 10, 5, 11, 4, 12, 3, 13, 2, 14, 1, 15):
        push(stat_mid, stat_z.at[k], stat_z_message[k], at_z(k))
    for k in range(1, NT):
        from_t = lax.rem(t - k + NT, NT)
        landed(logits_x.at[from_t], logits_message[k])
        landed(wx.at[from_t], w_message[k])
    wx[t] = wsend[t]
    for k in range(1, NZ):
        landed(stat_z.at[k], stat_z_message[k])
    top, row_total, pick = combine(stat_z, NZ)
    losses_ref[...] = top + jnp.log(row_total) - pick

    top_column = jnp.broadcast_to(top, (128, 128)).T
    total_column = jnp.broadcast_to(row_total, (128, 128)).T
    target_column = jnp.broadcast_to(target, (128, 128)).T
    lane = lax.broadcasted_iota(jnp.int32, (128, 128), 1)
    grads = []
    for i in range(NT):
        hit = (lane + (z * NT + i) * 128) == target_column
        grad = jnp.exp(logits_x[i] - top_column) / total_column - hit.astype(jnp.float32)
        grads.append(grad.astype(jnp.bfloat16))
    for q in range(4):
        part = jnp.zeros((128, 256), jnp.float32)
        for i in range(NT):
            part = part + jnp.dot(grads[i], wx[i, :, q * 256:(q + 1) * 256],
                                  preferred_element_type=jnp.float32)
        product[2 * q] = part[:, :128]
        product[2 * q + 1] = part[:, 128:]

    def piece(slot):
        there = lax.rem(z + OFFSETS[slot] + NZ, NZ)
        tile = product[there // 2]
        odd = lax.rem(there, 2) == 1
        upper, lower = tile[:64], tile[64:]
        even_piece = jnp.concatenate([upper[:, :64], lower[:, :64]], axis=1)
        odd_piece = jnp.concatenate([upper[:, 64:], lower[:, 64:]], axis=1)
        pieces[slot] = jnp.where(odd, odd_piece, even_piece)

    near_message = [new() for _ in NEAR]
    for i in (2, 3, 0, 1):
        for slot in range(4 + 3 * i, 7 + 3 * i):
            piece(slot)
        push(pieces.at[pl.ds(4 + 3 * i, 3)], near_sum.at[i], near_message[i], at_z(NEAR[i]))
    piece(3)
    opposite_message = new()
    push(pieces.at[3], opposite, opposite_message, at_z(8))
    for slot in range(3):
        piece(slot)

    own_grad = (jnp.exp(logits - top) / row_total - is_target.astype(jnp.float32)).astype(
        jnp.bfloat16)
    stores = []
    for q in range(4):
        for r in range(4):
            columns = pl.ds((4 * q + r) * 512, 512)
            d_w[:, columns] = jnp.dot(
                own_grad, full[:, columns], preferred_element_type=jnp.float32
            ).astype(jnp.bfloat16)
        columns = pl.ds(q * 2048, 2048)
        store = pltpu.make_async_copy(
            d_w.at[:, columns], d_weight_hbm.at[:, columns], local_sem.at[2 + q])
        store.start()
        stores.append(store)

    for i in range(4):
        landed(near_sum.at[i], near_message[i])
    far_message = [new(), new()]
    for slot in (1, 2, 0):
        pieces[slot] = (pieces[slot] + near_sum[0, slot] + near_sum[1, slot]
                        + near_sum[2, slot] + near_sum[3, slot])
        if slot:
            push(pieces.at[slot], far_sum.at[slot - 1], far_message[slot - 1],
                 at_z(OFFSETS[slot]))
    landed(opposite, opposite_message)
    landed(far_sum.at[0], far_message[0])
    landed(far_sum.at[1], far_message[1])
    result = (pieces[0] + opposite[...] + far_sum[0] + far_sum[1])
    d_hidden_ref[0:64, :] = result[:, :64].astype(jnp.bfloat16)
    d_hidden_ref[64:128, :] = result[:, 64:].astype(jnp.bfloat16)
    for store in stores:
        store.wait()
    for copy in sent:
        copy.wait_send()
    assert count[0] <= MESSAGES


def on_device(hidden, weight, targets):
    vmem = pl.BlockSpec(memory_space=pltpu.VMEM)
    anywhere = pl.BlockSpec(memory_space=pl.ANY)
    bf16, f32 = jnp.bfloat16, jnp.float32
    d_hidden, d_weight, losses = pl.pallas_call(
        kernel,
        out_shape=(
            jax.ShapeDtypeStruct((128, 64), bf16),
            jax.ShapeDtypeStruct((128, 8192), bf16),
            jax.ShapeDtypeStruct((1, 128), f32),
        ),
        in_specs=[anywhere, anywhere, vmem],
        out_specs=(vmem, anywhere, vmem),
        scratch_shapes=[
            pltpu.VMEM((128, 64), bf16),
            pltpu.VMEM((128, 8192), bf16),
            pltpu.VMEM((8, 128, 1024), bf16),
            pltpu.VMEM((8, 128, 1024), bf16),
            pltpu.VMEM((8, 16, 64, 128), bf16),
            pltpu.VMEM((128, 8192), bf16),
            pltpu.VMEM((8, 128, 128), f32),
            pltpu.VMEM((8, 1, 384), f32),
            pltpu.VMEM((16, 1, 384), f32),
            pltpu.VMEM((1, 384), f32),
            pltpu.VMEM((1, 384), f32),
            pltpu.VMEM((8, 128, 128), f32),
            pltpu.VMEM((16, 64, 128), f32),
            pltpu.VMEM((4, 3, 64, 128), f32),
            pltpu.VMEM((2, 64, 128), f32),
            pltpu.VMEM((64, 128), f32),
            pltpu.VMEM((128, 8192), bf16),
            pltpu.SemaphoreType.DMA((6,)),
            pltpu.SemaphoreType.DMA((MESSAGES,)),
            pltpu.SemaphoreType.DMA((MESSAGES,)),
        ],
        compiler_params=pltpu.CompilerParams(
            collective_id=0, has_side_effects=True, vmem_limit_bytes=48 * 2**20),
        cost_estimate=pl.CostEstimate(
            flops=3 * 2 * 128 * 128 * 8192, bytes_accessed=2 * 2 * 128 * 8192, transcendentals=0),
    )(hidden, weight, targets.reshape(1, 128))
    return d_hidden, d_weight, losses.reshape(128)


def solution(mesh):
    in_specs = (P("dp", ("pipe", "tensor")), P(("dp", "pipe", "tensor"), None), P("dp"))
    out_specs = (P("dp", ("pipe", "tensor")), P(("dp", "pipe", "tensor"), None), P("dp"))
    return jax.shard_map(
        on_device, mesh=mesh, in_specs=in_specs, out_specs=out_specs, check_vma=False
    )
```

```python
import jax
import jax.numpy as jnp
from jax import lax
from jax.experimental import pallas as pl
from jax.experimental.pallas import tpu as pltpu
from jax.sharding import PartitionSpec as P

MESH = pl.DeviceIdType.MESH
NZ, NX, NT = 16, 4, 8
NEAR = (1, -1, 2, -2)
OFFSETS = [0, 1, -1, 2, -2, 5, -5] + [b + a for b in NEAR for a in (5, -5)] + [8]
GROUPS = [(0, 5), (5, 2), (7, 9)]
OTHERS = [(k, e) for k in range(NX) for e in (0, 1)][1:]
MESSAGES = 128


def kernel(hidden_hbm, weight_hbm, targets_hbm, d_hidden_ref, d_weight_ref, losses_ref,
           targets_ref, w, wsend, wx, full, logits_x, exponents, stat_t, stat_z, stat_own, stat_mid,
           pieces, near_own, near_far, skip, far_sum, local_sem, send, recv):
    dp, z, t = lax.axis_index("dp"), lax.axis_index("pipe"), lax.axis_index("tensor")
    x, c = t // 2, lax.rem(t, 2)

    def z_at(offset):
        return lax.rem(z + offset + NZ, NZ)

    def at_z(offset):
        return (dp, z_at(offset), t)

    def t_at(k, e):
        return 2 * lax.rem(x + k + NX, NX) + lax.rem(c + e, 2)

    def at_t(k, e):
        return (dp, z, t_at(k, e))

    barrier = pltpu.get_barrier_semaphore()
    for k in (5, -5, 3, -3, 2, -2, 1, -1):
        pl.semaphore_signal(barrier, inc=1, device_id=at_z(k), device_id_type=MESH)
    for k, e in OTHERS:
        pl.semaphore_signal(barrier, inc=1, device_id=at_t(k, e), device_id_type=MESH)
    load_h = pltpu.make_async_copy(hidden_hbm, full.at[0, t], local_sem.at[0])
    load_w = pltpu.make_async_copy(weight_hbm, w, local_sem.at[1])
    load_targets = pltpu.make_async_copy(targets_hbm, targets_ref, local_sem.at[2])
    load_h.start()
    load_w.start()
    load_targets.start()

    count = [0]
    sent = []
    waited = set()

    def new():
        count[0] += 1
        return count[0] - 1

    def push(src, dst, k, device):
        copy = pltpu.make_async_remote_copy(
            src, dst, send.at[k], recv.at[k], device_id=device, device_id_type=MESH)
        copy.start()
        sent.append((k, copy))

    def landed(ref, k):
        waited.add(k)
        pltpu.make_async_remote_copy(
            ref, ref, send.at[k], recv.at[k], device_id=at_t(0, 1), device_id_type=MESH).wait_recv()

    load_h.wait()
    pl.semaphore_wait(barrier, 8 + NT - 1)

    own = full.at[0, t]
    own_message = [new() for _ in range(7)]
    for slot in (5, 6, 1, 2, 3, 4):
        push(own, full.at[slot, t], own_message[slot], at_z(-OFFSETS[slot]))

    w_message = {other: new() for other in OTHERS}

    def push_w(k, e):
        push(wsend.at[t_at(k, e)], wx.at[t], w_message[k, e], at_t(k, e))

    def turn_w(k):
        xx = lax.rem(x + k, NX)

        def body(j, _):
            tile = w[:, pl.ds(pl.multiple_of((j * NX + xx) * 128, 128), 128)].T
            wsend[2 * xx, j] = tile[:64]
            wsend[2 * xx + 1, j] = tile[64:]
            return 0
        lax.fori_loop(0, NZ, body, 0, unroll=4)

    x_message = [[None] + [new() for _ in range(NX - 1)] for _ in GROUPS]
    core_message = [[new() for _ in range(NX)] for _ in GROUPS]

    def push_x(g):
        start, size = GROUPS[g]
        part = full.at[pl.ds(start, size), t]
        for k in (2, 1, 3):
            push(part, part, x_message[g][k], at_t(k, 0))
        push(part, part, core_message[g][0], at_t(0, 1))

    def pass_on(g):
        start, size = GROUPS[g]
        for k in (1, 3, 2):
            part = full.at[pl.ds(start, size), t_at(-k, 0)]
            landed(part, x_message[g][k])
            push(part, part, core_message[g][k], at_t(0, 1))

    total = [jnp.zeros((128, 128), jnp.float32)]

    def absorb(g):
        start, size = GROUPS[g]
        for k in range(NX):
            landed(full.at[pl.ds(start, size), t_at(-k, 1)], core_message[g][k])
        for slot in range(start, start + size):
            columns = pl.ds(pl.multiple_of(z_at(OFFSETS[slot]) * 512, 512), 512)
            total[0] = total[0] + jnp.dot(
                w[:, columns], full[slot].reshape(512, 128), preferred_element_type=jnp.float32)

    load_w.wait()
    for k in (1, 3):
        turn_w(k)
        push_w(k, 0)
    for slot in range(1, 5):
        landed(full.at[slot, t], own_message[slot])
    push_x(0)
    for slot in (5, 6):
        landed(full.at[slot, t], own_message[slot])
    pair_message = [new() for _ in NEAR]
    half_message = [new(), new()]
    for i in (2, 3, 0, 1):
        push(full.at[pl.ds(5, 2), t], full.at[pl.ds(7 + 2 * i, 2), t], pair_message[i],
             at_z(-NEAR[i]))
    halves = (pl.ds(0, 32), pl.ds(32, 32))
    for i, offset in ((0, 3), (1, -3)):
        push(full.at[5 + i, t, halves[i]], full.at[15, t, halves[i]], half_message[i],
             at_z(-offset))
    push_x(1)
    turn_w(0)
    push_w(0, 1)
    turn_w(2)
    pass_on(0)
    absorb(0)
    for i in range(4):
        landed(full.at[pl.ds(7 + 2 * i, 2), t], pair_message[i])
    for i in range(2):
        landed(full.at[15, t, halves[i]], half_message[i])
    push_x(2)
    push_w(1, 1)
    push_w(3, 1)
    pass_on(1)
    absorb(1)
    wx[t] = wsend[t]
    pass_on(2)
    absorb(2)

    logits = total[0]
    row = lax.broadcasted_iota(jnp.int32, (128, 128), 0)
    load_targets.wait()
    target = targets_ref[...] - z * NT * 128
    top = jnp.max(logits, axis=0, keepdims=True)
    stat_own[:, 0:128] = top
    stat_own[:, 128:256] = jnp.sum(jnp.exp(logits - top), axis=0, keepdims=True)
    stat_own[:, 256:384] = jnp.sum(
        jnp.where(row + t * 128 == target, logits, 0.0), axis=0, keepdims=True)
    stat_t[0] = stat_own[...]
    stat_t_message = [new() for _ in OTHERS]
    for i in (3, 4, 1, 2, 5, 6, 0):
        push(stat_own, stat_t.at[i + 1], stat_t_message[i], at_t(*OTHERS[i]))
    logits_x[t] = logits
    logits_message = {other: new() for other in OTHERS}
    for k, e in ((2, 0), (1, 0), (3, 0), (0, 1)):
        push(logits_x.at[t], logits_x.at[t], logits_message[k, e], at_t(k, e))

    push_w(2, 0)
    push_w(2, 1)

    def combine(stats, n):
        top = stats[0, :, 0:128]
        for k in range(1, n):
            top = jnp.maximum(top, stats[k, :, 0:128])
        total = jnp.zeros_like(top)
        pick = jnp.zeros_like(top)
        for k in range(n):
            total = total + stats[k, :, 128:256] * jnp.exp(stats[k, :, 0:128] - top)
            pick = pick + stats[k, :, 256:384]
        return top, total, pick

    for i in range(NT - 1):
        landed(stat_t.at[i + 1], stat_t_message[i])
    group_top, row_total, pick = combine(stat_t, NT)
    stat_mid[:, 0:128] = group_top
    stat_mid[:, 128:256] = row_total
    stat_mid[:, 256:384] = pick
    stat_z[0] = stat_mid[...]
    stat_z_message = [None] + [new() for _ in range(NZ - 1)]
    for k in (8, 7, 9, 6, 10, 5, 11, 4, 12, 3, 13, 2, 14, 1, 15):
        push(stat_mid, stat_z.at[k], stat_z_message[k], at_z(k))
    for k in (1, 3, 2):
        part = logits_x.at[t_at(-k, 0)]
        landed(part, logits_message[k, 0])
        push(part, part, logits_message[k, 1], at_t(0, 1))
    landed(logits_x.at[t_at(0, 1)], logits_message[0, 1])
    for k in (1, 3, 2):
        landed(logits_x.at[t_at(-k, 1)], logits_message[k, 1])
    for i in range(NT):
        exponents[i] = jnp.exp(logits_x[i] - group_top)
    for k in range(1, NZ):
        landed(stat_z.at[k], stat_z_message[k])
    top, row_total, pick = combine(stat_z, NZ)
    losses_ref[...] = top + jnp.log(row_total) - pick
    factor = jnp.exp(group_top - top) / row_total

    grads = []
    for i in range(NT // 2):
        pair = []
        for j in (2 * i, 2 * i + 1):
            hit = (row + j * 128 == target).astype(jnp.float32)
            pair.append((exponents[j] * factor - hit).astype(jnp.bfloat16))
        grads.append(jnp.concatenate(pair, axis=0))
    for k, e in OTHERS:
        landed(wx.at[t_at(-k, e)], w_message[k, e])

    def contribute(slots):
        part = None
        for i in range(NT // 2):
            rows = [
                jnp.concatenate([wx[2 * i, z_at(OFFSETS[slot])],
                                 wx[2 * i + 1, z_at(OFFSETS[slot])]], axis=1)
                for slot in slots
            ]
            term = jnp.dot(jnp.concatenate(rows, axis=0), grads[i],
                           preferred_element_type=jnp.float32)
            part = term if part is None else part + term
        for n, slot in enumerate(slots):
            pieces[slot] = part[64 * n:64 * (n + 1)]

    far_pair_message = [new() for _ in NEAR]
    near_message = [new() for _ in NEAR]
    skip_message = [new(), new()]
    for i in (2, 3):
        contribute((7 + 2 * i, 8 + 2 * i))
        push(pieces.at[pl.ds(7 + 2 * i, 2)], near_far.at[i], far_pair_message[i], at_z(NEAR[i]))
    contribute((15,))
    for i, offset in ((0, 3), (1, -3)):
        push(pieces.at[15, halves[i]], skip.at[i], skip_message[i], at_z(offset))
    for i in (0, 1):
        contribute((7 + 2 * i, 8 + 2 * i))
        push(pieces.at[pl.ds(7 + 2 * i, 2)], near_far.at[i], far_pair_message[i], at_z(NEAR[i]))
    contribute((3, 4, 1, 2))
    for i in (2, 3, 0, 1):
        push(pieces.at[1 + i], near_own.at[i], near_message[i], at_z(NEAR[i]))
    contribute((5, 6, 0))

    own_hit = (row + t * 128 == target).astype(jnp.float32)
    own_grad = (exponents[t] * factor - own_hit).astype(jnp.bfloat16)

    def weight_gradient(slots):
        for slot in slots:
            columns = pl.ds(pl.multiple_of(z_at(OFFSETS[slot]) * 512, 512), 512)
            d_weight_ref[:, columns] = lax.dot_general(
                own_grad, full[slot].reshape(512, 128), (((1,), (1,)), ((), ())),
                preferred_element_type=jnp.float32).astype(jnp.bfloat16)

    weight_gradient(range(10))
    for i in range(4):
        landed(near_far.at[i], far_pair_message[i])
    for i in range(2):
        landed(skip.at[i], skip_message[i])
    far_message = [new(), new()]
    for i in (0, 1):
        pieces[5 + i] = (pieces[5 + i] + near_far[0, i] + near_far[1, i]
                         + near_far[2, i] + near_far[3, i])
        pieces[5 + i, halves[i]] += skip[i]
        push(pieces.at[5 + i], far_sum.at[i], far_message[i], at_z(OFFSETS[5 + i]))
    weight_gradient(range(10, NZ))
    for i in range(4):
        landed(near_own.at[i], near_message[i])
    landed(far_sum.at[0], far_message[0])
    landed(far_sum.at[1], far_message[1])
    d_hidden_ref[...] = (pieces[0] + near_own[0] + near_own[1] + near_own[2] + near_own[3]
                         + far_sum[0] + far_sum[1]).astype(jnp.bfloat16)
    for _, copy in sent:
        copy.wait_send()
    assert count[0] <= MESSAGES


def on_device(hidden, weight, targets):
    vmem = pl.BlockSpec(memory_space=pltpu.VMEM)
    hbm = pl.BlockSpec(memory_space=pltpu.HBM)
    bf16, f32 = jnp.bfloat16, jnp.float32
    d_hidden, d_weight, losses = pl.pallas_call(
        kernel,
        out_shape=(
            jax.ShapeDtypeStruct((64, 128), bf16),
            jax.ShapeDtypeStruct((128, 8192), bf16),
            jax.ShapeDtypeStruct((1, 128), f32),
        ),
        in_specs=[hbm, hbm, hbm],
        out_specs=(vmem, vmem, vmem),
        scratch_shapes=[
            pltpu.VMEM((1, 128), jnp.int32),
            pltpu.VMEM((128, 8192), bf16),
            pltpu.VMEM((8, 16, 64, 128), bf16),
            pltpu.VMEM((8, 16, 64, 128), bf16),
            pltpu.VMEM((16, 8, 64, 128), bf16),
            pltpu.VMEM((8, 128, 128), f32),
            pltpu.VMEM((8, 128, 128), f32),
            pltpu.VMEM((8, 1, 384), f32),
            pltpu.VMEM((16, 1, 384), f32),
            pltpu.VMEM((1, 384), f32),
            pltpu.VMEM((1, 384), f32),
            pltpu.VMEM((16, 64, 128), f32),
            pltpu.VMEM((4, 64, 128), f32),
            pltpu.VMEM((4, 2, 64, 128), f32),
            pltpu.VMEM((2, 32, 128), f32),
            pltpu.VMEM((2, 64, 128), f32),
            pltpu.SemaphoreType.DMA((3,)),
            pltpu.SemaphoreType.DMA((MESSAGES,)),
            pltpu.SemaphoreType.DMA((MESSAGES,)),
        ],
        compiler_params=pltpu.CompilerParams(
            collective_id=0, has_side_effects=True, vmem_limit_bytes=50 * 2**20),
        cost_estimate=pl.CostEstimate(
            flops=3 * 2 * 128 * 128 * 8192, bytes_accessed=2 * 2 * 128 * 8192, transcendentals=0),
    )(hidden.T, weight, targets.reshape(1, 128))
    return d_hidden.T, d_weight, losses.reshape(128)


def solution(mesh):
    in_specs = (P("dp", ("pipe", "tensor")), P(("dp", "pipe", "tensor"), None), P("dp"))
    out_specs = (P("dp", ("pipe", "tensor")), P(("dp", "pipe", "tensor"), None), P("dp"))
    return jax.shard_map(
        on_device, mesh=mesh, in_specs=in_specs, out_specs=out_specs, check_vma=False
    )
```

```python
import jax
import jax.numpy as jnp
from jax import lax
from jax.experimental import pallas as pl
from jax.experimental.pallas import tpu as pltpu
from jax.sharding import PartitionSpec as P

MESH = pl.DeviceIdType.MESH
NZ, NX, NT = 16, 4, 8
NEAR = (1, -1, 2, -2)
OFFSETS = [0, 1, -1, 2, -2, 5, -5] + [b + a for b in NEAR for a in (5, -5)] + [8]
GROUPS = [(0, 5), (5, 2), (7, 9)]
OTHERS = [(k, e) for k in range(NX) for e in (0, 1)][1:]
MESSAGES = 128


def kernel(hidden_hbm, weight_hbm, targets_hbm, d_hidden_ref, d_weight_ref, losses_ref,
           targets_ref, w, wsend, wx, along_z, along_x, logits_x, exponents, stat_t, stat_z, stat_own, stat_mid,
           pieces, near_own, near_far, skip, far_sum, local_sem, send, recv):
    dp, z, t = lax.axis_index("dp"), lax.axis_index("pipe"), lax.axis_index("tensor")
    x, c = t // 2, lax.rem(t, 2)

    def z_at(offset):
        return lax.rem(z + offset + NZ, NZ)

    def at_z(offset):
        return (dp, z_at(offset), t)

    def t_at(k, e):
        return 2 * lax.rem(x + k + NX, NX) + lax.rem(c + e, 2)

    def at_t(k, e):
        return (dp, z, t_at(k, e))

    barrier = pltpu.get_barrier_semaphore()
    for k in (5, -5, 3, -3, 2, -2, 1, -1):
        pl.semaphore_signal(barrier, inc=1, device_id=at_z(k), device_id_type=MESH)
    for k, e in OTHERS:
        pl.semaphore_signal(barrier, inc=1, device_id=at_t(k, e), device_id_type=MESH)
    load_a = pltpu.make_async_copy(hidden_hbm.at[pl.ds(0, 32)], along_z.at[0, t], local_sem.at[0])
    load_b = pltpu.make_async_copy(
        hidden_hbm.at[pl.ds(32, 32)], along_x.at[0, c, x], local_sem.at[3])
    load_w = pltpu.make_async_copy(weight_hbm, w, local_sem.at[1])
    load_targets = pltpu.make_async_copy(targets_hbm, targets_ref, local_sem.at[2])
    load_a.start()
    load_b.start()
    load_w.start()
    load_targets.start()

    count = [0]
    sent = []
    waited = set()

    def new():
        count[0] += 1
        return count[0] - 1

    def push(src, dst, k, device):
        copy = pltpu.make_async_remote_copy(
            src, dst, send.at[k], recv.at[k], device_id=device, device_id_type=MESH)
        copy.start()
        sent.append((k, copy))

    def landed(ref, k):
        waited.add(k)
        pltpu.make_async_remote_copy(
            ref, ref, send.at[k], recv.at[k], device_id=at_t(0, 1), device_id_type=MESH).wait_recv()

    load_a.wait()
    load_b.wait()
    pl.semaphore_wait(barrier, 8 + NT - 1)

    spread_message = [new() for _ in range(NX)]
    for k in (2, 1, 3):
        part = along_x.at[0, c, x]
        push(part, part, spread_message[k], at_t(k, 0))
    own_message = [new() for _ in range(7)]
    for slot in (5, 6, 1, 2, 3, 4):
        push(along_z.at[0, t], along_z.at[slot, t], own_message[slot], at_z(-OFFSETS[slot]))

    w_message = {other: new() for other in OTHERS}

    def push_w(k, e):
        push(wsend.at[t_at(k, e)], wx.at[t], w_message[k, e], at_t(k, e))

    def turn_w(k):
        xx = lax.rem(x + k, NX)

        def body(j, _):
            tile = w[:, pl.ds(pl.multiple_of((j * NX + xx) * 128, 128), 128)].T
            wsend[2 * xx, j] = tile[:64]
            wsend[2 * xx + 1, j] = tile[64:]
            return 0
        lax.fori_loop(0, NZ, body, 0, unroll=4)

    x_message = [[None] + [new() for _ in range(NX - 1)] for _ in GROUPS]
    core_message = [[new() for _ in range(NX)] for _ in GROUPS]

    def push_x(g):
        start, size = GROUPS[g]
        part = along_z.at[pl.ds(start, size), t]
        for k in (2, 1, 3):
            push(part, part, x_message[g][k], at_t(k, 0))
        push(part, part, core_message[g][0], at_t(0, 1))

    def pass_on(g):
        start, size = GROUPS[g]
        for k in (1, 3, 2):
            part = along_z.at[pl.ds(start, size), t_at(-k, 0)]
            landed(part, x_message[g][k])
            push(part, part, core_message[g][k], at_t(0, 1))

    def block(slot):
        rows = []
        for xx in range(NX):
            for cc in (0, 1):
                rows.append(along_z[slot, 2 * xx + cc])
                rows.append(along_x[slot, cc, xx])
        return jnp.concatenate(rows, axis=0)

    total = [jnp.zeros((128, 128), jnp.float32)]

    def absorb(g):
        start, size = GROUPS[g]
        for k in range(NX):
            landed(along_z.at[pl.ds(start, size), t_at(-k, 1)], core_message[g][k])
        for slot in range(start, start + size):
            columns = pl.ds(pl.multiple_of(z_at(OFFSETS[slot]) * 512, 512), 512)
            total[0] = total[0] + jnp.dot(
                w[:, columns], block(slot), preferred_element_type=jnp.float32)

    load_w.wait()
    for k in (1, 3):
        turn_w(k)
        push_w(k, 0)
    for k in (1, 3, 2):
        landed(along_x.at[0, c, lax.rem(x - k + NX, NX)], spread_message[k])
    wide_message = [new() for _ in range(7)]
    for slot in (5, 6, 1, 2, 3, 4):
        push(along_x.at[0, c], along_x.at[slot, c], wide_message[slot], at_z(-OFFSETS[slot]))
    for slot in range(1, 5):
        landed(along_z.at[slot, t], own_message[slot])
    push_x(0)
    push_w(1, 1)
    push_w(3, 1)
    for slot in (5, 6):
        landed(along_z.at[slot, t], own_message[slot])
    pair_message = [new() for _ in NEAR]
    half_message = [new(), new()]
    for i in (2, 3, 0, 1):
        push(along_z.at[pl.ds(5, 2), t], along_z.at[pl.ds(7 + 2 * i, 2), t], pair_message[i],
             at_z(-NEAR[i]))
    halves = (pl.ds(0, 16), pl.ds(16, 16))
    for i, offset in ((0, 3), (1, -3)):
        push(along_z.at[5 + i, t, halves[i]], along_z.at[15, t, halves[i]], half_message[i],
             at_z(-offset))
    push_x(1)
    turn_w(0)
    push_w(0, 1)
    turn_w(2)
    for slot in (5, 6):
        landed(along_x.at[slot, c], wide_message[slot])
    wide_pair_message = [new() for _ in NEAR]
    wide_half_message = [new(), new()]
    for i in (2, 3, 0, 1):
        push(along_x.at[pl.ds(5, 2), c], along_x.at[pl.ds(7 + 2 * i, 2), c],
             wide_pair_message[i], at_z(-NEAR[i]))
    wide_halves = (pl.ds(0, 2), pl.ds(2, 2))
    for i, offset in ((0, 3), (1, -3)):
        push(along_x.at[5 + i, c, wide_halves[i]], along_x.at[15, c, wide_halves[i]],
             wide_half_message[i], at_z(-offset))
    for slot in range(1, 5):
        landed(along_x.at[slot, c], wide_message[slot])
    wide_core_message = [new(), new()]
    part = along_x.at[pl.ds(0, 7), c]
    push(part, part, wide_core_message[0], at_t(0, 1))
    pass_on(0)
    for i in range(4):
        landed(along_z.at[pl.ds(7 + 2 * i, 2), t], pair_message[i])
    for i in range(2):
        landed(along_z.at[15, t, halves[i]], half_message[i])
    push_x(2)
    push_w(2, 0)
    pass_on(1)
    landed(along_x.at[pl.ds(0, 7), 1 - c], wide_core_message[0])
    absorb(0)
    absorb(1)
    for i in range(4):
        landed(along_x.at[pl.ds(7 + 2 * i, 2), c], wide_pair_message[i])
    for i in range(2):
        landed(along_x.at[15, c, wide_halves[i]], wide_half_message[i])
    part = along_x.at[pl.ds(7, 9), c]
    push(part, part, wide_core_message[1], at_t(0, 1))
    pass_on(2)
    wx[t] = wsend[t]
    landed(along_x.at[pl.ds(7, 9), 1 - c], wide_core_message[1])
    absorb(2)

    logits = total[0]
    row = lax.broadcasted_iota(jnp.int32, (128, 128), 0)
    load_targets.wait()
    target = targets_ref[...] - z * NT * 128
    top = jnp.max(logits, axis=0, keepdims=True)
    stat_own[:, 0:128] = top
    stat_own[:, 128:256] = jnp.sum(jnp.exp(logits - top), axis=0, keepdims=True)
    stat_own[:, 256:384] = jnp.sum(
        jnp.where(row + t * 128 == target, logits, 0.0), axis=0, keepdims=True)
    stat_t[0] = stat_own[...]
    stat_t_message = [new() for _ in OTHERS]
    for i in (3, 4, 1, 2, 5, 6, 0):
        push(stat_own, stat_t.at[i + 1], stat_t_message[i], at_t(*OTHERS[i]))
    logits_x[t] = logits
    logits_message = {other: new() for other in OTHERS}
    for k, e in ((2, 0), (1, 0), (3, 0), (0, 1)):
        push(logits_x.at[t], logits_x.at[t], logits_message[k, e], at_t(k, e))

    push_w(2, 1)

    def combine(stats, n):
        top = stats[0, :, 0:128]
        for k in range(1, n):
            top = jnp.maximum(top, stats[k, :, 0:128])
        total = jnp.zeros_like(top)
        pick = jnp.zeros_like(top)
        for k in range(n):
            total = total + stats[k, :, 128:256] * jnp.exp(stats[k, :, 0:128] - top)
            pick = pick + stats[k, :, 256:384]
        return top, total, pick

    for i in range(NT - 1):
        landed(stat_t.at[i + 1], stat_t_message[i])
    group_top, row_total, pick = combine(stat_t, NT)
    stat_mid[:, 0:128] = group_top
    stat_mid[:, 128:256] = row_total
    stat_mid[:, 256:384] = pick
    stat_z[0] = stat_mid[...]
    stat_z_message = [None] + [new() for _ in range(NZ - 1)]
    for k in (8, 7, 9, 6, 10, 5, 11, 4, 12, 3, 13, 2, 14, 1, 15):
        push(stat_mid, stat_z.at[k], stat_z_message[k], at_z(k))
    for k in (1, 3, 2):
        part = logits_x.at[t_at(-k, 0)]
        landed(part, logits_message[k, 0])
        push(part, part, logits_message[k, 1], at_t(0, 1))
    landed(logits_x.at[t_at(0, 1)], logits_message[0, 1])
    for k in (1, 3, 2):
        landed(logits_x.at[t_at(-k, 1)], logits_message[k, 1])
    for i in range(NT):
        exponents[i] = jnp.exp(logits_x[i] - group_top)
    for k in range(1, NZ):
        landed(stat_z.at[k], stat_z_message[k])
    top, row_total, pick = combine(stat_z, NZ)
    losses_ref[...] = top + jnp.log(row_total) - pick
    factor = jnp.exp(group_top - top) / row_total

    grads = []
    for i in range(NT // 2):
        pair = []
        for j in (2 * i, 2 * i + 1):
            hit = (row + j * 128 == target).astype(jnp.float32)
            pair.append((exponents[j] * factor - hit).astype(jnp.bfloat16))
        grads.append(jnp.concatenate(pair, axis=0))
    for k, e in OTHERS:
        landed(wx.at[t_at(-k, e)], w_message[k, e])

    def contribute(slots):
        part = None
        for i in range(NT // 2):
            rows = [
                jnp.concatenate([wx[2 * i, z_at(OFFSETS[slot])],
                                 wx[2 * i + 1, z_at(OFFSETS[slot])]], axis=1)
                for slot in slots
            ]
            term = jnp.dot(jnp.concatenate(rows, axis=0), grads[i],
                           preferred_element_type=jnp.float32)
            part = term if part is None else part + term
        for n, slot in enumerate(slots):
            pieces[slot] = part[64 * n:64 * (n + 1)]

    sum_halves = (pl.ds(0, 32), pl.ds(32, 32))
    far_pair_message = [new() for _ in NEAR]
    near_message = [new() for _ in NEAR]
    skip_message = [new(), new()]
    for i in (2, 3):
        contribute((7 + 2 * i, 8 + 2 * i))
        push(pieces.at[pl.ds(7 + 2 * i, 2)], near_far.at[i], far_pair_message[i], at_z(NEAR[i]))
    contribute((15,))
    for i, offset in ((0, 3), (1, -3)):
        push(pieces.at[15, sum_halves[i]], skip.at[i], skip_message[i], at_z(offset))
    for i in (0, 1):
        contribute((7 + 2 * i, 8 + 2 * i))
        push(pieces.at[pl.ds(7 + 2 * i, 2)], near_far.at[i], far_pair_message[i], at_z(NEAR[i]))
    contribute((3, 4, 1, 2))
    for i in (2, 3, 0, 1):
        push(pieces.at[1 + i], near_own.at[i], near_message[i], at_z(NEAR[i]))
    contribute((5, 6, 0))

    own_hit = (row + t * 128 == target).astype(jnp.float32)
    own_grad = (exponents[t] * factor - own_hit).astype(jnp.bfloat16)

    def weight_gradient(slots):
        for slot in slots:
            columns = pl.ds(pl.multiple_of(z_at(OFFSETS[slot]) * 512, 512), 512)
            d_weight_ref[:, columns] = lax.dot_general(
                own_grad, block(slot), (((1,), (1,)), ((), ())),
                preferred_element_type=jnp.float32).astype(jnp.bfloat16)

    weight_gradient(range(10))
    for i in range(4):
        landed(near_far.at[i], far_pair_message[i])
    for i in range(2):
        landed(skip.at[i], skip_message[i])
    far_message = [new(), new()]
    for i in (0, 1):
        pieces[5 + i] = (pieces[5 + i] + near_far[0, i] + near_far[1, i]
                         + near_far[2, i] + near_far[3, i])
        pieces[5 + i, sum_halves[i]] += skip[i]
        push(pieces.at[5 + i], far_sum.at[i], far_message[i], at_z(OFFSETS[5 + i]))
    weight_gradient(range(10, NZ))
    for i in range(4):
        landed(near_own.at[i], near_message[i])
    landed(far_sum.at[0], far_message[0])
    landed(far_sum.at[1], far_message[1])
    d_hidden_ref[...] = (pieces[0] + near_own[0] + near_own[1] + near_own[2] + near_own[3]
                         + far_sum[0] + far_sum[1]).astype(jnp.bfloat16)
    for _, copy in sent:
        copy.wait_send()
    assert count[0] <= MESSAGES


def on_device(hidden, weight, targets):
    vmem = pl.BlockSpec(memory_space=pltpu.VMEM)
    hbm = pl.BlockSpec(memory_space=pltpu.HBM)
    bf16, f32 = jnp.bfloat16, jnp.float32
    d_hidden, d_weight, losses = pl.pallas_call(
        kernel,
        out_shape=(
            jax.ShapeDtypeStruct((64, 128), bf16),
            jax.ShapeDtypeStruct((128, 8192), bf16),
            jax.ShapeDtypeStruct((1, 128), f32),
        ),
        in_specs=[hbm, hbm, hbm],
        out_specs=(vmem, vmem, vmem),
        scratch_shapes=[
            pltpu.VMEM((1, 128), jnp.int32),
            pltpu.VMEM((128, 8192), bf16),
            pltpu.VMEM((8, 16, 64, 128), bf16),
            pltpu.VMEM((8, 16, 64, 128), bf16),
            pltpu.VMEM((16, 8, 32, 128), bf16),
            pltpu.VMEM((16, 2, 4, 32, 128), bf16),
            pltpu.VMEM((8, 128, 128), f32),
            pltpu.VMEM((8, 128, 128), f32),
            pltpu.VMEM((8, 1, 384), f32),
            pltpu.VMEM((16, 1, 384), f32),
            pltpu.VMEM((1, 384), f32),
            pltpu.VMEM((1, 384), f32),
            pltpu.VMEM((16, 64, 128), f32),
            pltpu.VMEM((4, 64, 128), f32),
            pltpu.VMEM((4, 2, 64, 128), f32),
            pltpu.VMEM((2, 32, 128), f32),
            pltpu.VMEM((2, 64, 128), f32),
            pltpu.SemaphoreType.DMA((4,)),
            pltpu.SemaphoreType.DMA((MESSAGES,)),
            pltpu.SemaphoreType.DMA((MESSAGES,)),
        ],
        compiler_params=pltpu.CompilerParams(
            collective_id=0, has_side_effects=True, vmem_limit_bytes=50 * 2**20),
        cost_estimate=pl.CostEstimate(
            flops=3 * 2 * 128 * 128 * 8192, bytes_accessed=2 * 2 * 128 * 8192, transcendentals=0),
    )(hidden.T, weight, targets.reshape(1, 128))
    return d_hidden.T, d_weight, losses.reshape(128)


def solution(mesh):
    in_specs = (P("dp", ("pipe", "tensor")), P(("dp", "pipe", "tensor"), None), P("dp"))
    out_specs = (P("dp", ("pipe", "tensor")), P(("dp", "pipe", "tensor"), None), P("dp"))
    return jax.shard_map(
        on_device, mesh=mesh, in_specs=in_specs, out_specs=out_specs, check_vma=False
    )
```

```python
import jax
import jax.numpy as jnp
from jax import lax
from jax.experimental import pallas as pl
from jax.experimental.pallas import tpu as pltpu
from jax.sharding import PartitionSpec as P

MESH = pl.DeviceIdType.MESH
NZ, NX, NT = 16, 4, 8
NEAR = (1, -1, 2, -2)
OFFSETS = [0, 1, -1, 2, -2, 5, -5] + [b + a for b in NEAR for a in (5, -5)] + [8]
GROUPS = [(0, 5), (5, 2), (7, 9)]
OTHERS = [(k, e) for k in range(NX) for e in (0, 1)][1:]
MESSAGES = 128


def kernel(hidden_hbm, weight_hbm, targets_hbm, d_hidden_ref, d_weight_ref, losses_ref,
           targets_ref, w, wsend, wx, along_z, along_x, logits_x, exponents, stat_t, stat_z, stat_own, stat_mid,
           pieces, near_own, near_far, skip, far_sum, local_sem, send, recv):
    dp, z, t = lax.axis_index("dp"), lax.axis_index("pipe"), lax.axis_index("tensor")
    x, c = t // 2, lax.rem(t, 2)

    def z_at(offset):
        return lax.rem(z + offset + NZ, NZ)

    def at_z(offset):
        return (dp, z_at(offset), t)

    def t_at(k, e):
        return 2 * lax.rem(x + k + NX, NX) + lax.rem(c + e, 2)

    def at_t(k, e):
        return (dp, z, t_at(k, e))

    barrier = pltpu.get_barrier_semaphore()
    for k in (5, -5, 3, -3, 2, -2, 1, -1):
        pl.semaphore_signal(barrier, inc=1, device_id=at_z(k), device_id_type=MESH)
    for k, e in OTHERS:
        pl.semaphore_signal(barrier, inc=1, device_id=at_t(k, e), device_id_type=MESH)
    load_a = pltpu.make_async_copy(hidden_hbm.at[pl.ds(0, 32)], along_z.at[0, t], local_sem.at[0])
    load_b = pltpu.make_async_copy(
        hidden_hbm.at[pl.ds(32, 32)], along_x.at[0, c, x], local_sem.at[3])
    load_w = pltpu.make_async_copy(weight_hbm, w, local_sem.at[1])
    load_targets = pltpu.make_async_copy(targets_hbm, targets_ref, local_sem.at[2])
    load_a.start()
    load_b.start()
    load_w.start()
    load_targets.start()

    count = [0]
    sent = []
    waited = set()

    def new():
        count[0] += 1
        return count[0] - 1

    def push(src, dst, k, device):
        copy = pltpu.make_async_remote_copy(
            src, dst, send.at[k], recv.at[k], device_id=device, device_id_type=MESH)
        copy.start()
        sent.append((k, copy))

    def landed(ref, k):
        waited.add(k)
        pltpu.make_async_remote_copy(
            ref, ref, send.at[k], recv.at[k], device_id=at_t(0, 1), device_id_type=MESH).wait_recv()

    load_a.wait()
    load_b.wait()
    pl.semaphore_wait(barrier, 8 + NT - 1)

    spread_message = [new() for _ in range(NX)]
    for k in (2, 1, 3):
        part = along_x.at[0, c, x]
        push(part, part, spread_message[k], at_t(k, 0))
    own_message = [new() for _ in range(7)]
    for slot in (5, 6, 1, 2, 3, 4):
        push(along_z.at[0, t], along_z.at[slot, t], own_message[slot], at_z(-OFFSETS[slot]))

    w_message = {other: new() for other in OTHERS}

    def push_w(k, e):
        push(wsend.at[t_at(k, e)], wx.at[t], w_message[k, e], at_t(k, e))

    def turn_w(k):
        xx = lax.rem(x + k, NX)

        def body(j, _):
            tile = w[:, pl.ds(pl.multiple_of((j * NX + xx) * 128, 128), 128)].T
            wsend[2 * xx, j] = tile[:64]
            wsend[2 * xx + 1, j] = tile[64:]
            return 0
        lax.fori_loop(0, NZ, body, 0, unroll=4)

    x_message = [[None] + [new() for _ in range(NX - 1)] for _ in GROUPS]
    core_message = [[new() for _ in range(NX)] for _ in GROUPS]

    def push_x(g):
        start, size = GROUPS[g]
        part = along_z.at[pl.ds(start, size), t]
        for k in (2, 1, 3):
            push(part, part, x_message[g][k], at_t(k, 0))
        push(part, part, core_message[g][0], at_t(0, 1))

    def pass_on(g):
        start, size = GROUPS[g]
        for k in (1, 3, 2):
            part = along_z.at[pl.ds(start, size), t_at(-k, 0)]
            landed(part, x_message[g][k])
            push(part, part, core_message[g][k], at_t(0, 1))

    def block(slot):
        rows = []
        for xx in range(NX):
            for cc in (0, 1):
                rows.append(along_z[slot, 2 * xx + cc])
                rows.append(along_x[slot, cc, xx])
        return jnp.concatenate(rows, axis=0)

    total = [jnp.zeros((128, 128), jnp.float32)]

    def absorb(g):
        start, size = GROUPS[g]
        for k in range(NX):
            landed(along_z.at[pl.ds(start, size), t_at(-k, 1)], core_message[g][k])
        for slot in range(start, start + size):
            columns = pl.ds(pl.multiple_of(z_at(OFFSETS[slot]) * 512, 512), 512)
            total[0] = total[0] + jnp.dot(
                w[:, columns], block(slot), preferred_element_type=jnp.float32)

    load_w.wait()
    for k in (1, 3):
        turn_w(k)
        push_w(k, 0)
    for k in (1, 3, 2):
        landed(along_x.at[0, c, lax.rem(x - k + NX, NX)], spread_message[k])
    wide_message = [new() for _ in range(7)]
    for slot in (5, 6, 1, 2, 3, 4):
        push(along_x.at[0, c], along_x.at[slot, c], wide_message[slot], at_z(-OFFSETS[slot]))
    for slot in range(1, 5):
        landed(along_z.at[slot, t], own_message[slot])
    push_x(0)
    push_w(1, 1)
    push_w(3, 1)
    for slot in (5, 6):
        landed(along_z.at[slot, t], own_message[slot])
    pair_message = [new() for _ in NEAR]
    half_message = [new(), new()]
    for i in (2, 3, 0, 1):
        push(along_z.at[pl.ds(5, 2), t], along_z.at[pl.ds(7 + 2 * i, 2), t], pair_message[i],
             at_z(-NEAR[i]))
    halves = (pl.ds(0, 16), pl.ds(16, 16))
    for i, offset in ((0, 3), (1, -3)):
        push(along_z.at[5 + i, t, halves[i]], along_z.at[15, t, halves[i]], half_message[i],
             at_z(-offset))
    push_x(1)
    turn_w(0)
    push_w(0, 1)
    turn_w(2)
    for slot in (5, 6):
        landed(along_x.at[slot, c], wide_message[slot])
    wide_pair_message = [new() for _ in NEAR]
    wide_half_message = [new(), new()]
    for i in (2, 3, 0, 1):
        push(along_x.at[pl.ds(5, 2), c], along_x.at[pl.ds(7 + 2 * i, 2), c],
             wide_pair_message[i], at_z(-NEAR[i]))
    wide_halves = (pl.ds(0, 2), pl.ds(2, 2))
    for i, offset in ((0, 3), (1, -3)):
        push(along_x.at[5 + i, c, wide_halves[i]], along_x.at[15, c, wide_halves[i]],
             wide_half_message[i], at_z(-offset))
    for slot in range(1, 5):
        landed(along_x.at[slot, c], wide_message[slot])
    wide_core_message = [new(), new()]
    part = along_x.at[pl.ds(0, 7), c]
    push(part, part, wide_core_message[0], at_t(0, 1))
    pass_on(0)
    for i in range(4):
        landed(along_z.at[pl.ds(7 + 2 * i, 2), t], pair_message[i])
    for i in range(2):
        landed(along_z.at[15, t, halves[i]], half_message[i])
    push_x(2)
    push_w(2, 0)
    pass_on(1)
    landed(along_x.at[pl.ds(0, 7), 1 - c], wide_core_message[0])
    absorb(0)
    absorb(1)
    for i in range(4):
        landed(along_x.at[pl.ds(7 + 2 * i, 2), c], wide_pair_message[i])
    for i in range(2):
        landed(along_x.at[15, c, wide_halves[i]], wide_half_message[i])
    part = along_x.at[pl.ds(7, 9), c]
    push(part, part, wide_core_message[1], at_t(0, 1))
    pass_on(2)
    wx[t] = wsend[t]
    landed(along_x.at[pl.ds(7, 9), 1 - c], wide_core_message[1])
    absorb(2)

    logits = total[0]
    row = lax.broadcasted_iota(jnp.int32, (128, 128), 0)
    load_targets.wait()
    target = targets_ref[...] - z * NT * 128
    top = jnp.max(logits, axis=0, keepdims=True)
    stat_own[:, 0:128] = top
    stat_own[:, 128:256] = jnp.sum(jnp.exp(logits - top), axis=0, keepdims=True)
    stat_own[:, 256:384] = jnp.sum(
        jnp.where(row + t * 128 == target, logits, 0.0), axis=0, keepdims=True)
    stat_t[0] = stat_own[...]
    stat_t_message = [new() for _ in OTHERS]
    for i in (3, 4, 1, 2, 5, 6, 0):
        push(stat_own, stat_t.at[i + 1], stat_t_message[i], at_t(*OTHERS[i]))
    logits_x[t] = logits
    logits_message = {other: new() for other in OTHERS}
    for k, e in ((2, 0), (1, 0), (3, 0), (0, 1)):
        push(logits_x.at[t], logits_x.at[t], logits_message[k, e], at_t(k, e))

    push_w(2, 1)

    def combine(stats, n):
        top = stats[0, :, 0:128]
        for k in range(1, n):
            top = jnp.maximum(top, stats[k, :, 0:128])
        total = jnp.zeros_like(top)
        pick = jnp.zeros_like(top)
        for k in range(n):
            total = total + stats[k, :, 128:256] * jnp.exp(stats[k, :, 0:128] - top)
            pick = pick + stats[k, :, 256:384]
        return top, total, pick

    for i in range(NT - 1):
        landed(stat_t.at[i + 1], stat_t_message[i])
    group_top, row_total, pick = combine(stat_t, NT)
    stat_mid[:, 0:128] = group_top
    stat_mid[:, 128:256] = row_total
    stat_mid[:, 256:384] = pick
    stat_z[0] = stat_mid[...]
    stat_z_message = [None] + [new() for _ in range(NZ - 1)]
    for k in (8, 7, 9, 6, 10, 5, 11, 4, 12, 3, 13, 2, 14, 1, 15):
        push(stat_mid, stat_z.at[k], stat_z_message[k], at_z(k))
    for k in (1, 3, 2):
        part = logits_x.at[t_at(-k, 0)]
        landed(part, logits_message[k, 0])
        push(part, part, logits_message[k, 1], at_t(0, 1))
    landed(logits_x.at[t_at(0, 1)], logits_message[0, 1])
    for k in (1, 3, 2):
        landed(logits_x.at[t_at(-k, 1)], logits_message[k, 1])
    for i in range(NT):
        exponents[i] = jnp.exp(logits_x[i] - group_top)
    for k in range(1, NZ):
        landed(stat_z.at[k], stat_z_message[k])
    top, row_total, pick = combine(stat_z, NZ)
    losses_ref[...] = top + jnp.log(row_total) - pick
    factor = jnp.exp(group_top - top) / row_total

    grads = []
    for i in range(NT // 2):
        pair = []
        for j in (2 * i, 2 * i + 1):
            hit = (row + j * 128 == target).astype(jnp.float32)
            pair.append((exponents[j] * factor - hit).astype(jnp.bfloat16))
        grads.append(jnp.concatenate(pair, axis=0))
    for k, e in OTHERS:
        landed(wx.at[t_at(-k, e)], w_message[k, e])

    def contribute(slots):
        part = None
        for i in range(NT // 2):
            rows = [
                jnp.concatenate([wx[2 * i, z_at(OFFSETS[slot])],
                                 wx[2 * i + 1, z_at(OFFSETS[slot])]], axis=1)
                for slot in slots
            ]
            term = jnp.dot(jnp.concatenate(rows, axis=0), grads[i],
                           preferred_element_type=jnp.float32)
            part = term if part is None else part + term
        for n, slot in enumerate(slots):
            pieces[slot] = part[64 * n:64 * (n + 1)]

    sum_halves = (pl.ds(0, 32), pl.ds(32, 32))
    far_pair_message = [new() for _ in NEAR]
    near_message = [new() for _ in NEAR]
    skip_message = [new(), new()]
    for i in (2, 3):
        contribute((7 + 2 * i, 8 + 2 * i))
        push(pieces.at[pl.ds(7 + 2 * i, 2)], near_far.at[i], far_pair_message[i], at_z(NEAR[i]))
    contribute((15,))
    for i, offset in ((0, 3), (1, -3)):
        push(pieces.at[15, sum_halves[i]], skip.at[i], skip_message[i], at_z(offset))
    for i in (0, 1):
        contribute((7 + 2 * i, 8 + 2 * i))
        push(pieces.at[pl.ds(7 + 2 * i, 2)], near_far.at[i], far_pair_message[i], at_z(NEAR[i]))
    contribute((3, 4, 1, 2))
    for i in (2, 3, 0, 1):
        push(pieces.at[1 + i], near_own.at[i], near_message[i], at_z(NEAR[i]))
    contribute((5, 6, 0))

    own_hit = (row + t * 128 == target).astype(jnp.float32)
    own_grad = (exponents[t] * factor - own_hit).astype(jnp.bfloat16)

    def weight_gradient(slots):
        for slot in slots:
            columns = pl.ds(pl.multiple_of(z_at(OFFSETS[slot]) * 512, 512), 512)
            d_weight_ref[:, columns] = lax.dot_general(
                own_grad, block(slot), (((1,), (1,)), ((), ())),
                preferred_element_type=jnp.float32).astype(jnp.bfloat16)

    weight_gradient(range(10))
    for i in range(4):
        landed(near_far.at[i], far_pair_message[i])
    for i in range(2):
        landed(skip.at[i], skip_message[i])
    far_message = [new(), new()]
    for i in (0, 1):
        pieces[5 + i] = (pieces[5 + i] + near_far[0, i] + near_far[1, i]
                         + near_far[2, i] + near_far[3, i])
        pieces[5 + i, sum_halves[i]] += skip[i]
        push(pieces.at[5 + i], far_sum.at[i], far_message[i], at_z(OFFSETS[5 + i]))
    weight_gradient(range(10, NZ))
    for i in range(4):
        landed(near_own.at[i], near_message[i])
    landed(far_sum.at[0], far_message[0])
    landed(far_sum.at[1], far_message[1])
    d_hidden_ref[...] = (pieces[0] + near_own[0] + near_own[1] + near_own[2] + near_own[3]
                         + far_sum[0] + far_sum[1]).astype(jnp.bfloat16)
    for _, copy in sent:
        copy.wait_send()
    assert count[0] <= MESSAGES


def deliver(a_ref, b_ref, c_ref, a_out, b_out, c_out, sem):
    copies = [
        pltpu.make_async_copy(b_ref, b_out, sem.at[0]),
        pltpu.make_async_copy(a_ref, a_out, sem.at[1]),
        pltpu.make_async_copy(c_ref, c_out, sem.at[2]),
    ]
    for copy in copies:
        copy.start()
    for copy in copies:
        copy.wait()


def on_device(hidden, weight, targets):
    vmem = pl.BlockSpec(memory_space=pltpu.VMEM)
    hbm = pl.BlockSpec(memory_space=pltpu.HBM)
    bf16, f32 = jnp.bfloat16, jnp.float32
    d_hidden, d_weight, losses = pl.pallas_call(
        kernel,
        out_shape=(
            jax.ShapeDtypeStruct((64, 128), bf16),
            jax.ShapeDtypeStruct((128, 8192), bf16),
            jax.ShapeDtypeStruct((1, 128), f32),
        ),
        in_specs=[hbm, hbm, hbm],
        out_specs=(vmem, vmem, vmem),
        scratch_shapes=[
            pltpu.VMEM((1, 128), jnp.int32),
            pltpu.VMEM((128, 8192), bf16),
            pltpu.VMEM((8, 16, 64, 128), bf16),
            pltpu.VMEM((8, 16, 64, 128), bf16),
            pltpu.VMEM((16, 8, 32, 128), bf16),
            pltpu.VMEM((16, 2, 4, 32, 128), bf16),
            pltpu.VMEM((8, 128, 128), f32),
            pltpu.VMEM((8, 128, 128), f32),
            pltpu.VMEM((8, 1, 384), f32),
            pltpu.VMEM((16, 1, 384), f32),
            pltpu.VMEM((1, 384), f32),
            pltpu.VMEM((1, 384), f32),
            pltpu.VMEM((16, 64, 128), f32),
            pltpu.VMEM((4, 64, 128), f32),
            pltpu.VMEM((4, 2, 64, 128), f32),
            pltpu.VMEM((2, 32, 128), f32),
            pltpu.VMEM((2, 64, 128), f32),
            pltpu.SemaphoreType.DMA((4,)),
            pltpu.SemaphoreType.DMA((MESSAGES,)),
            pltpu.SemaphoreType.DMA((MESSAGES,)),
        ],
        compiler_params=pltpu.CompilerParams(
            collective_id=0, has_side_effects=True, vmem_limit_bytes=50 * 2**20),
        cost_estimate=pl.CostEstimate(
            flops=3 * 2 * 128 * 128 * 8192, bytes_accessed=2 * 2 * 128 * 8192, transcendentals=0),
    )(hidden.T, weight, targets.reshape(1, 128))
    d_hidden, d_weight, losses = pl.pallas_call(
        deliver,
        out_shape=(
            jax.ShapeDtypeStruct((64, 128), bf16),
            jax.ShapeDtypeStruct((128, 8192), bf16),
            jax.ShapeDtypeStruct((1, 128), f32),
        ),
        in_specs=[pl.BlockSpec(memory_space=pl.ANY)] * 3,
        out_specs=[pl.BlockSpec(memory_space=pl.ANY)] * 3,
        scratch_shapes=[pltpu.SemaphoreType.DMA((3,))],
        compiler_params=pltpu.CompilerParams(vmem_limit_bytes=8 * 2**20),
        cost_estimate=pl.CostEstimate(
            flops=0, bytes_accessed=2 * 2 * 128 * 8192, transcendentals=0),
    )(d_hidden, d_weight, losses)
    return d_hidden.T, d_weight, losses.reshape(128)


def solution(mesh):
    in_specs = (P("dp", ("pipe", "tensor")), P(("dp", "pipe", "tensor"), None), P("dp"))
    out_specs = (P("dp", ("pipe", "tensor")), P(("dp", "pipe", "tensor"), None), P("dp"))
    return jax.shard_map(
        on_device, mesh=mesh, in_specs=in_specs, out_specs=out_specs, check_vma=False
    )
```

```python
import jax
import jax.numpy as jnp
from jax import lax
from jax.experimental import pallas as pl
from jax.experimental.pallas import tpu as pltpu
from jax.sharding import PartitionSpec as P

MESH = pl.DeviceIdType.MESH
NZ, NX, NT = 16, 4, 8
NEAR = (1, -1, 2, -2)
OFFSETS = [0, 1, -1, 2, -2, 5, -5] + [b + a for b in NEAR for a in (5, -5)] + [8]
GROUPS = [(0, 5), (5, 2), (7, 9)]
OTHERS = [(k, e) for k in range(NX) for e in (0, 1)][1:]
MESSAGES = 128


def kernel(hidden_hbm, weight_hbm, targets_hbm, d_hidden_ref, d_weight_ref, losses_ref,
           targets_ref, w, wsend, wx, along_z, along_x, logits_x, exponents, stat_t, stat_z, stat_own, stat_mid,
           pieces, near_own, near_far, skip, far_sum, local_sem, send, recv):
    dp, z, t = lax.axis_index("dp"), lax.axis_index("pipe"), lax.axis_index("tensor")
    x, c = t // 2, lax.rem(t, 2)

    def z_at(offset):
        return lax.rem(z + offset + NZ, NZ)

    def at_z(offset):
        return (dp, z_at(offset), t)

    def t_at(k, e):
        return 2 * lax.rem(x + k + NX, NX) + lax.rem(c + e, 2)

    def at_t(k, e):
        return (dp, z, t_at(k, e))

    barrier = pltpu.get_barrier_semaphore()
    for k in (5, -5, 3, -3, 2, -2, 1, -1):
        pl.semaphore_signal(barrier, inc=1, device_id=at_z(k), device_id_type=MESH)
    for k, e in OTHERS:
        pl.semaphore_signal(barrier, inc=1, device_id=at_t(k, e), device_id_type=MESH)
    load_a = pltpu.make_async_copy(hidden_hbm.at[pl.ds(0, 16)], along_z.at[0, t], local_sem.at[0])
    load_b = pltpu.make_async_copy(
        hidden_hbm.at[pl.ds(16, 48)], along_x.at[0, c, x], local_sem.at[3])
    load_w = pltpu.make_async_copy(weight_hbm, w, local_sem.at[1])
    load_targets = pltpu.make_async_copy(targets_hbm, targets_ref, local_sem.at[2])
    load_a.start()
    load_b.start()
    load_w.start()
    load_targets.start()

    count = [0]
    sent = []
    waited = set()

    def new():
        count[0] += 1
        return count[0] - 1

    def push(src, dst, k, device):
        copy = pltpu.make_async_remote_copy(
            src, dst, send.at[k], recv.at[k], device_id=device, device_id_type=MESH)
        copy.start()
        sent.append((k, copy))

    def landed(ref, k):
        waited.add(k)
        pltpu.make_async_remote_copy(
            ref, ref, send.at[k], recv.at[k], device_id=at_t(0, 1), device_id_type=MESH).wait_recv()

    load_a.wait()
    load_b.wait()
    pl.semaphore_wait(barrier, 8 + NT - 1)

    spread_message = [new() for _ in range(NX)]
    for k in (2, 1, 3):
        part = along_x.at[0, c, x]
        push(part, part, spread_message[k], at_t(k, 0))
    own_message = [new() for _ in range(7)]
    for slot in (5, 6, 1, 2, 3, 4):
        push(along_z.at[0, t], along_z.at[slot, t], own_message[slot], at_z(-OFFSETS[slot]))

    w_message = {other: new() for other in OTHERS}

    def push_w(k, e):
        push(wsend.at[t_at(k, e)], wx.at[t], w_message[k, e], at_t(k, e))

    def turn_w(k):
        xx = lax.rem(x + k, NX)

        def body(j, _):
            tile = w[:, pl.ds(pl.multiple_of((j * NX + xx) * 128, 128), 128)].T
            wsend[2 * xx, j] = tile[:64]
            wsend[2 * xx + 1, j] = tile[64:]
            return 0
        lax.fori_loop(0, NZ, body, 0, unroll=4)

    x_message = [[None] + [new() for _ in range(NX - 1)] for _ in GROUPS]
    core_message = [[new() for _ in range(NX)] for _ in GROUPS]

    def push_x(g):
        start, size = GROUPS[g]
        part = along_z.at[pl.ds(start, size), t]
        for k in (2, 1, 3):
            push(part, part, x_message[g][k], at_t(k, 0))
        push(part, part, core_message[g][0], at_t(0, 1))

    def pass_on(g):
        start, size = GROUPS[g]
        for k in (1, 3, 2):
            part = along_z.at[pl.ds(start, size), t_at(-k, 0)]
            landed(part, x_message[g][k])
            push(part, part, core_message[g][k], at_t(0, 1))

    def block(slot):
        rows = []
        for xx in range(NX):
            for cc in (0, 1):
                rows.append(along_z[slot, 2 * xx + cc])
                rows.append(along_x[slot, cc, xx])
        return jnp.concatenate(rows, axis=0)

    total = [jnp.zeros((128, 128), jnp.float32)]

    def absorb(g):
        start, size = GROUPS[g]
        for k in range(NX):
            landed(along_z.at[pl.ds(start, size), t_at(-k, 1)], core_message[g][k])
        for slot in range(start, start + size):
            columns = pl.ds(pl.multiple_of(z_at(OFFSETS[slot]) * 512, 512), 512)
            total[0] = total[0] + jnp.dot(
                w[:, columns], block(slot), preferred_element_type=jnp.float32)

    load_w.wait()
    for k in (1, 3):
        turn_w(k)
        push_w(k, 0)
    for k in (1, 3, 2):
        landed(along_x.at[0, c, lax.rem(x - k + NX, NX)], spread_message[k])
    wide_message = [new() for _ in range(7)]
    for slot in (5, 6, 1, 2, 3, 4):
        push(along_x.at[0, c], along_x.at[slot, c], wide_message[slot], at_z(-OFFSETS[slot]))
    for slot in range(1, 5):
        landed(along_z.at[slot, t], own_message[slot])
    push_x(0)
    push_w(1, 1)
    push_w(3, 1)
    for slot in (5, 6):
        landed(along_z.at[slot, t], own_message[slot])
    pair_message = [new() for _ in NEAR]
    skip_block_message = new()
    for i in (2, 3, 0, 1):
        push(along_z.at[pl.ds(5, 2), t], along_z.at[pl.ds(7 + 2 * i, 2), t], pair_message[i],
             at_z(-NEAR[i]))
    push(along_z.at[5, t], along_z.at[15, t], skip_block_message, at_z(-3))
    push_x(1)
    turn_w(0)
    push_w(0, 1)
    turn_w(2)
    for slot in (5, 6):
        landed(along_x.at[slot, c], wide_message[slot])
    wide_pair_message = [new() for _ in NEAR]
    wide_half_message = [new(), new()]
    for i in (2, 3, 0, 1):
        push(along_x.at[pl.ds(5, 2), c], along_x.at[pl.ds(7 + 2 * i, 2), c],
             wide_pair_message[i], at_z(-NEAR[i]))
    wide_halves = (pl.ds(0, 2), pl.ds(2, 2))
    for i, offset in ((0, 3), (1, -3)):
        push(along_x.at[5 + i, c, wide_halves[i]], along_x.at[15, c, wide_halves[i]],
             wide_half_message[i], at_z(-offset))
    for slot in range(1, 5):
        landed(along_x.at[slot, c], wide_message[slot])
    wide_core_message = [new(), new()]
    part = along_x.at[pl.ds(0, 7), c]
    push(part, part, wide_core_message[0], at_t(0, 1))
    pass_on(0)
    for i in range(4):
        landed(along_z.at[pl.ds(7 + 2 * i, 2), t], pair_message[i])
    landed(along_z.at[15, t], skip_block_message)
    push_x(2)
    push_w(2, 0)
    pass_on(1)
    landed(along_x.at[pl.ds(0, 7), 1 - c], wide_core_message[0])
    absorb(0)
    absorb(1)
    for i in range(4):
        landed(along_x.at[pl.ds(7 + 2 * i, 2), c], wide_pair_message[i])
    for i in range(2):
        landed(along_x.at[15, c, wide_halves[i]], wide_half_message[i])
    part = along_x.at[pl.ds(7, 9), c]
    push(part, part, wide_core_message[1], at_t(0, 1))
    pass_on(2)
    wx[t] = wsend[t]
    landed(along_x.at[pl.ds(7, 9), 1 - c], wide_core_message[1])
    absorb(2)

    logits = total[0]
    row = lax.broadcasted_iota(jnp.int32, (128, 128), 0)
    load_targets.wait()
    target = targets_ref[...] - z * NT * 128
    top = jnp.max(logits, axis=0, keepdims=True)
    stat_own[:, 0:128] = top
    stat_own[:, 128:256] = jnp.sum(jnp.exp(logits - top), axis=0, keepdims=True)
    stat_own[:, 256:384] = jnp.sum(
        jnp.where(row + t * 128 == target, logits, 0.0), axis=0, keepdims=True)
    stat_t[0] = stat_own[...]
    stat_t_message = [new() for _ in OTHERS]
    for i in (3, 4, 1, 2, 5, 6, 0):
        push(stat_own, stat_t.at[i + 1], stat_t_message[i], at_t(*OTHERS[i]))
    logits_x[t] = logits
    logits_message = {other: new() for other in OTHERS}
    for k, e in ((2, 0), (1, 0), (3, 0), (0, 1)):
        push(logits_x.at[t], logits_x.at[t], logits_message[k, e], at_t(k, e))

    push_w(2, 1)

    def combine(stats, n):
        top = stats[0, :, 0:128]
        for k in range(1, n):
            top = jnp.maximum(top, stats[k, :, 0:128])
        total = jnp.zeros_like(top)
        pick = jnp.zeros_like(top)
        for k in range(n):
            total = total + stats[k, :, 128:256] * jnp.exp(stats[k, :, 0:128] - top)
            pick = pick + stats[k, :, 256:384]
        return top, total, pick

    for i in range(NT - 1):
        landed(stat_t.at[i + 1], stat_t_message[i])
    group_top, row_total, pick = combine(stat_t, NT)
    stat_mid[:, 0:128] = group_top
    stat_mid[:, 128:256] = row_total
    stat_mid[:, 256:384] = pick
    stat_z[0] = stat_mid[...]
    stat_z_message = [None] + [new() for _ in range(NZ - 1)]
    for k in (8, 7, 9, 6, 10, 5, 11, 4, 12, 3, 13, 2, 14, 1, 15):
        push(stat_mid, stat_z.at[k], stat_z_message[k], at_z(k))
    for k in (1, 3, 2):
        part = logits_x.at[t_at(-k, 0)]
        landed(part, logits_message[k, 0])
        push(part, part, logits_message[k, 1], at_t(0, 1))
    landed(logits_x.at[t_at(0, 1)], logits_message[0, 1])
    for k in (1, 3, 2):
        landed(logits_x.at[t_at(-k, 1)], logits_message[k, 1])
    for i in range(NT):
        exponents[i] = jnp.exp(logits_x[i] - group_top)
    for k in range(1, NZ):
        landed(stat_z.at[k], stat_z_message[k])
    top, row_total, pick = combine(stat_z, NZ)
    losses_ref[...] = top + jnp.log(row_total) - pick
    factor = jnp.exp(group_top - top) / row_total

    grads = []
    for i in range(NT // 2):
        pair = []
        for j in (2 * i, 2 * i + 1):
            hit = (row + j * 128 == target).astype(jnp.float32)
            pair.append((exponents[j] * factor - hit).astype(jnp.bfloat16))
        grads.append(jnp.concatenate(pair, axis=0))
    for k, e in OTHERS:
        landed(wx.at[t_at(-k, e)], w_message[k, e])

    def contribute(slots):
        part = None
        for i in range(NT // 2):
            rows = [
                jnp.concatenate([wx[2 * i, z_at(OFFSETS[slot])],
                                 wx[2 * i + 1, z_at(OFFSETS[slot])]], axis=1)
                for slot in slots
            ]
            term = jnp.dot(jnp.concatenate(rows, axis=0), grads[i],
                           preferred_element_type=jnp.float32)
            part = term if part is None else part + term
        for n, slot in enumerate(slots):
            pieces[slot] = part[64 * n:64 * (n + 1)]

    sum_halves = (pl.ds(0, 32), pl.ds(32, 32))
    far_pair_message = [new() for _ in NEAR]
    near_message = [new() for _ in NEAR]
    skip_message = [new(), new()]
    for i in (2, 3):
        contribute((7 + 2 * i, 8 + 2 * i))
        push(pieces.at[pl.ds(7 + 2 * i, 2)], near_far.at[i], far_pair_message[i], at_z(NEAR[i]))
    contribute((15,))
    for i, offset in ((0, 3), (1, -3)):
        push(pieces.at[15, sum_halves[i]], skip.at[i], skip_message[i], at_z(offset))
    for i in (0, 1):
        contribute((7 + 2 * i, 8 + 2 * i))
        push(pieces.at[pl.ds(7 + 2 * i, 2)], near_far.at[i], far_pair_message[i], at_z(NEAR[i]))
    contribute((3, 4, 1, 2))
    for i in (2, 3, 0, 1):
        push(pieces.at[1 + i], near_own.at[i], near_message[i], at_z(NEAR[i]))
    contribute((5, 6, 0))

    own_hit = (row + t * 128 == target).astype(jnp.float32)
    own_grad = (exponents[t] * factor - own_hit).astype(jnp.bfloat16)

    def weight_gradient(slots):
        for slot in slots:
            columns = pl.ds(pl.multiple_of(z_at(OFFSETS[slot]) * 512, 512), 512)
            d_weight_ref[:, columns] = lax.dot_general(
                own_grad, block(slot), (((1,), (1,)), ((), ())),
                preferred_element_type=jnp.float32).astype(jnp.bfloat16)

    weight_gradient(range(10))
    for i in range(4):
        landed(near_far.at[i], far_pair_message[i])
    for i in range(2):
        landed(skip.at[i], skip_message[i])
    far_message = [new(), new()]
    for i in (0, 1):
        pieces[5 + i] = (pieces[5 + i] + near_far[0, i] + near_far[1, i]
                         + near_far[2, i] + near_far[3, i])
        pieces[5 + i, sum_halves[i]] += skip[i]
        push(pieces.at[5 + i], far_sum.at[i], far_message[i], at_z(OFFSETS[5 + i]))
    weight_gradient(range(10, NZ))
    for i in range(4):
        landed(near_own.at[i], near_message[i])
    landed(far_sum.at[0], far_message[0])
    landed(far_sum.at[1], far_message[1])
    d_hidden_ref[...] = (pieces[0] + near_own[0] + near_own[1] + near_own[2] + near_own[3]
                         + far_sum[0] + far_sum[1]).astype(jnp.bfloat16)
    for _, copy in sent:
        copy.wait_send()
    assert count[0] <= MESSAGES


def deliver(a_ref, b_ref, c_ref, a_out, b_out, c_out, sem):
    copies = [
        pltpu.make_async_copy(b_ref, b_out, sem.at[0]),
        pltpu.make_async_copy(a_ref, a_out, sem.at[1]),
        pltpu.make_async_copy(c_ref, c_out, sem.at[2]),
    ]
    for copy in copies:
        copy.start()
    for copy in copies:
        copy.wait()


def on_device(hidden, weight, targets):
    vmem = pl.BlockSpec(memory_space=pltpu.VMEM)
    hbm = pl.BlockSpec(memory_space=pltpu.HBM)
    bf16, f32 = jnp.bfloat16, jnp.float32
    d_hidden, d_weight, losses = pl.pallas_call(
        kernel,
        out_shape=(
            jax.ShapeDtypeStruct((64, 128), bf16),
            jax.ShapeDtypeStruct((128, 8192), bf16),
            jax.ShapeDtypeStruct((1, 128), f32),
        ),
        in_specs=[hbm, hbm, hbm],
        out_specs=(vmem, vmem, vmem),
        scratch_shapes=[
            pltpu.VMEM((1, 128), jnp.int32),
            pltpu.VMEM((128, 8192), bf16),
            pltpu.VMEM((8, 16, 64, 128), bf16),
            pltpu.VMEM((8, 16, 64, 128), bf16),
            pltpu.VMEM((16, 8, 16, 128), bf16),
            pltpu.VMEM((16, 2, 4, 48, 128), bf16),
            pltpu.VMEM((8, 128, 128), f32),
            pltpu.VMEM((8, 128, 128), f32),
            pltpu.VMEM((8, 1, 384), f32),
            pltpu.VMEM((16, 1, 384), f32),
            pltpu.VMEM((1, 384), f32),
            pltpu.VMEM((1, 384), f32),
            pltpu.VMEM((16, 64, 128), f32),
            pltpu.VMEM((4, 64, 128), f32),
            pltpu.VMEM((4, 2, 64, 128), f32),
            pltpu.VMEM((2, 32, 128), f32),
            pltpu.VMEM((2, 64, 128), f32),
            pltpu.SemaphoreType.DMA((4,)),
            pltpu.SemaphoreType.DMA((MESSAGES,)),
            pltpu.SemaphoreType.DMA((MESSAGES,)),
        ],
        compiler_params=pltpu.CompilerParams(
            collective_id=0, has_side_effects=True, vmem_limit_bytes=50 * 2**20),
        cost_estimate=pl.CostEstimate(
            flops=3 * 2 * 128 * 128 * 8192, bytes_accessed=2 * 2 * 128 * 8192, transcendentals=0),
    )(hidden.T, weight, targets.reshape(1, 128))
    d_hidden, d_weight, losses = pl.pallas_call(
        deliver,
        out_shape=(
            jax.ShapeDtypeStruct((64, 128), bf16),
            jax.ShapeDtypeStruct((128, 8192), bf16),
            jax.ShapeDtypeStruct((1, 128), f32),
        ),
        in_specs=[pl.BlockSpec(memory_space=pl.ANY)] * 3,
        out_specs=[pl.BlockSpec(memory_space=pl.ANY)] * 3,
        scratch_shapes=[pltpu.SemaphoreType.DMA((3,))],
        compiler_params=pltpu.CompilerParams(vmem_limit_bytes=8 * 2**20),
        cost_estimate=pl.CostEstimate(
            flops=0, bytes_accessed=2 * 2 * 128 * 8192, transcendentals=0),
    )(d_hidden, d_weight, losses)
    return d_hidden.T, d_weight, losses.reshape(128)


def solution(mesh):
    in_specs = (P("dp", ("pipe", "tensor")), P(("dp", "pipe", "tensor"), None), P("dp"))
    out_specs = (P("dp", ("pipe", "tensor")), P(("dp", "pipe", "tensor"), None), P("dp"))
    return jax.shard_map(
        on_device, mesh=mesh, in_specs=in_specs, out_specs=out_specs, check_vma=False
    )
```

```python
import jax
import jax.numpy as jnp
from jax import lax
from jax.experimental import pallas as pl
from jax.experimental.pallas import tpu as pltpu
from jax.sharding import PartitionSpec as P

MESH = pl.DeviceIdType.MESH
NZ, NX, NT = 16, 4, 8
NEAR = (1, -1, 2, -2)
OFFSETS = [0, 1, -1, 2, -2, 5, -5] + [b + a for b in NEAR for a in (5, -5)] + [8]
GROUPS = [(0, 5), (5, 2), (7, 9)]
OTHERS = [(k, e) for k in range(NX) for e in (0, 1)][1:]
MESSAGES = 128


def kernel(hidden_hbm, weight_hbm, targets_hbm, d_hidden_ref, d_weight_ref, losses_ref,
           targets_ref, w, wsend, wx, along_z, along_x, logits_x, exponents, stat_t, stat_z, stat_own, stat_mid,
           pieces, near_own, near_far, skip, far_sum, local_sem, send, recv):
    dp, z, t = lax.axis_index("dp"), lax.axis_index("pipe"), lax.axis_index("tensor")
    x, c = t // 2, lax.rem(t, 2)

    def z_at(offset):
        return lax.rem(z + offset + NZ, NZ)

    def at_z(offset):
        return (dp, z_at(offset), t)

    def t_at(k, e):
        return 2 * lax.rem(x + k + NX, NX) + lax.rem(c + e, 2)

    def at_t(k, e):
        return (dp, z, t_at(k, e))

    barrier = pltpu.get_barrier_semaphore()
    for k in (5, -5, 3, -3, 2, -2, 1, -1):
        pl.semaphore_signal(barrier, inc=1, device_id=at_z(k), device_id_type=MESH)
    for k, e in OTHERS:
        pl.semaphore_signal(barrier, inc=1, device_id=at_t(k, e), device_id_type=MESH)
    load_a = pltpu.make_async_copy(hidden_hbm.at[pl.ds(0, 32)], along_z.at[0, t], local_sem.at[0])
    load_b = pltpu.make_async_copy(
        hidden_hbm.at[pl.ds(32, 32)], along_x.at[0, c, x], local_sem.at[3])
    load_w = pltpu.make_async_copy(weight_hbm, w, local_sem.at[1])
    load_targets = pltpu.make_async_copy(targets_hbm, targets_ref, local_sem.at[2])
    load_a.start()
    load_b.start()
    load_w.start()
    load_targets.start()

    count = [0]
    sent = []
    waited = set()

    def new():
        count[0] += 1
        return count[0] - 1

    def push(src, dst, k, device):
        copy = pltpu.make_async_remote_copy(
            src, dst, send.at[k], recv.at[k], device_id=device, device_id_type=MESH)
        copy.start()
        sent.append((k, copy))

    def landed(ref, k):
        waited.add(k)
        pltpu.make_async_remote_copy(
            ref, ref, send.at[k], recv.at[k], device_id=at_t(0, 1), device_id_type=MESH).wait_recv()

    load_a.wait()
    load_b.wait()
    pl.semaphore_wait(barrier, 8 + NT - 1)

    spread_message = [new() for _ in range(NX)]
    for k in (2, 1, 3):
        part = along_x.at[0, c, x]
        push(part, part, spread_message[k], at_t(k, 0))
    own_message = [new() for _ in range(7)]
    for slot in (5, 6, 1, 2, 3, 4):
        push(along_z.at[0, t], along_z.at[slot, t], own_message[slot], at_z(-OFFSETS[slot]))

    w_message = {other: new() for other in OTHERS}

    def push_w(k, e):
        push(wsend.at[t_at(k, e)], wx.at[t], w_message[k, e], at_t(k, e))

    def turn_w(k):
        xx = lax.rem(x + k, NX)

        def body(j, _):
            tile = w[:, pl.ds(pl.multiple_of((j * NX + xx) * 128, 128), 128)].T
            wsend[2 * xx, j] = tile[:64]
            wsend[2 * xx + 1, j] = tile[64:]
            return 0
        lax.fori_loop(0, NZ, body, 0, unroll=4)

    x_message = [[None] + [new() for _ in range(NX - 1)] for _ in GROUPS]
    core_message = [[new() for _ in range(NX)] for _ in GROUPS]

    def push_x(g):
        start, size = GROUPS[g]
        part = along_z.at[pl.ds(start, size), t]
        for k in (2, 1, 3):
            push(part, part, x_message[g][k], at_t(k, 0))
        push(part, part, core_message[g][0], at_t(0, 1))

    def pass_on(g):
        start, size = GROUPS[g]
        for k in (1, 3, 2):
            part = along_z.at[pl.ds(start, size), t_at(-k, 0)]
            landed(part, x_message[g][k])
            push(part, part, core_message[g][k], at_t(0, 1))

    def block(slot):
        rows = []
        for xx in range(NX):
            for cc in (0, 1):
                rows.append(along_z[slot, 2 * xx + cc])
                rows.append(along_x[slot, cc, xx])
        return jnp.concatenate(rows, axis=0)

    total = [jnp.zeros((128, 128), jnp.float32)]

    def absorb(g):
        start, size = GROUPS[g]
        for k in range(NX):
            landed(along_z.at[pl.ds(start, size), t_at(-k, 1)], core_message[g][k])
        for slot in range(start, start + size):
            columns = pl.ds(pl.multiple_of(z_at(OFFSETS[slot]) * 512, 512), 512)
            total[0] = total[0] + jnp.dot(
                w[:, columns], block(slot), preferred_element_type=jnp.float32)

    load_w.wait()
    for k in (1, 3):
        turn_w(k)
        push_w(k, 0)
    for k in (1, 3, 2):
        landed(along_x.at[0, c, lax.rem(x - k + NX, NX)], spread_message[k])
    wide_message = [new() for _ in range(7)]
    for slot in (5, 6, 1, 2, 3, 4):
        push(along_x.at[0, c], along_x.at[slot, c], wide_message[slot], at_z(-OFFSETS[slot]))
    for slot in range(1, 5):
        landed(along_z.at[slot, t], own_message[slot])
    push_x(0)
    push_w(1, 1)
    push_w(3, 1)
    for slot in (5, 6):
        landed(along_z.at[slot, t], own_message[slot])
    pair_message = [new() for _ in NEAR]
    half_message = [new(), new()]
    for i in (2, 3, 0, 1):
        push(along_z.at[pl.ds(5, 2), t], along_z.at[pl.ds(7 + 2 * i, 2), t], pair_message[i],
             at_z(-NEAR[i]))
    halves = (pl.ds(0, 16), pl.ds(16, 16))
    for i, offset in ((0, 3), (1, -3)):
        push(along_z.at[5 + i, t, halves[i]], along_z.at[15, t, halves[i]], half_message[i],
             at_z(-offset))
    push_x(1)
    turn_w(0)
    push_w(0, 1)
    turn_w(2)
    for slot in (5, 6):
        landed(along_x.at[slot, c], wide_message[slot])
    wide_pair_message = [new() for _ in NEAR]
    wide_half_message = [new(), new()]
    for i in (2, 3, 0, 1):
        push(along_x.at[pl.ds(5, 2), c], along_x.at[pl.ds(7 + 2 * i, 2), c],
             wide_pair_message[i], at_z(-NEAR[i]))
    wide_halves = (pl.ds(0, 2), pl.ds(2, 2))
    for i, offset in ((0, 3), (1, -3)):
        push(along_x.at[5 + i, c, wide_halves[i]], along_x.at[15, c, wide_halves[i]],
             wide_half_message[i], at_z(-offset))
    for slot in range(1, 5):
        landed(along_x.at[slot, c], wide_message[slot])
    wide_core_message = [new(), new()]
    part = along_x.at[pl.ds(0, 7), c]
    push(part, part, wide_core_message[0], at_t(0, 1))
    pass_on(0)
    for i in range(4):
        landed(along_z.at[pl.ds(7 + 2 * i, 2), t], pair_message[i])
    for i in range(2):
        landed(along_z.at[15, t, halves[i]], half_message[i])
    push_x(2)
    push_w(2, 0)
    pass_on(1)
    landed(along_x.at[pl.ds(0, 7), 1 - c], wide_core_message[0])
    absorb(0)
    absorb(1)
    pass_on(2)
    early, late = pl.ds(0, 4), pl.ds(4, 12)
    early_message = new()
    push(wsend.at[t_at(2, 1), early], wx.at[t, early], early_message, at_t(2, 1))
    for i in range(4):
        landed(along_x.at[pl.ds(7 + 2 * i, 2), c], wide_pair_message[i])
    for i in range(2):
        landed(along_x.at[15, c, wide_halves[i]], wide_half_message[i])
    part = along_x.at[pl.ds(7, 9), c]
    push(part, part, wide_core_message[1], at_t(0, 1))
    wx[t] = wsend[t]
    landed(along_x.at[pl.ds(7, 9), 1 - c], wide_core_message[1])
    absorb(2)

    logits = total[0]
    row = lax.broadcasted_iota(jnp.int32, (128, 128), 0)
    load_targets.wait()
    target = targets_ref[...] - z * NT * 128
    top = jnp.max(logits, axis=0, keepdims=True)
    stat_own[:, 0:128] = top
    stat_own[:, 128:256] = jnp.sum(jnp.exp(logits - top), axis=0, keepdims=True)
    stat_own[:, 256:384] = jnp.sum(
        jnp.where(row + t * 128 == target, logits, 0.0), axis=0, keepdims=True)
    stat_t[0] = stat_own[...]
    stat_t_message = [new() for _ in OTHERS]
    for i in (3, 4, 1, 2, 5, 6, 0):
        push(stat_own, stat_t.at[i + 1], stat_t_message[i], at_t(*OTHERS[i]))
    logits_x[t] = logits
    logits_message = {other: new() for other in OTHERS}
    for k, e in ((2, 0), (1, 0), (3, 0), (0, 1)):
        push(logits_x.at[t], logits_x.at[t], logits_message[k, e], at_t(k, e))

    push(wsend.at[t_at(2, 1), late], wx.at[t, late], w_message[2, 1], at_t(2, 1))

    def combine(stats, n):
        top = stats[0, :, 0:128]
        for k in range(1, n):
            top = jnp.maximum(top, stats[k, :, 0:128])
        total = jnp.zeros_like(top)
        pick = jnp.zeros_like(top)
        for k in range(n):
            total = total + stats[k, :, 128:256] * jnp.exp(stats[k, :, 0:128] - top)
            pick = pick + stats[k, :, 256:384]
        return top, total, pick

    for i in range(NT - 1):
        landed(stat_t.at[i + 1], stat_t_message[i])
    group_top, row_total, pick = combine(stat_t, NT)
    stat_mid[:, 0:128] = group_top
    stat_mid[:, 128:256] = row_total
    stat_mid[:, 256:384] = pick
    stat_z[0] = stat_mid[...]
    stat_z_message = [None] + [new() for _ in range(NZ - 1)]
    for k in (8, 7, 9, 6, 10, 5, 11, 4, 12, 3, 13, 2, 14, 1, 15):
        push(stat_mid, stat_z.at[k], stat_z_message[k], at_z(k))
    for k in (1, 3, 2):
        part = logits_x.at[t_at(-k, 0)]
        landed(part, logits_message[k, 0])
        push(part, part, logits_message[k, 1], at_t(0, 1))
    landed(logits_x.at[t_at(0, 1)], logits_message[0, 1])
    for k in (1, 3, 2):
        landed(logits_x.at[t_at(-k, 1)], logits_message[k, 1])
    for i in range(NT):
        exponents[i] = jnp.exp(logits_x[i] - group_top)
    for k in range(1, NZ):
        landed(stat_z.at[k], stat_z_message[k])
    top, row_total, pick = combine(stat_z, NZ)
    losses_ref[...] = top + jnp.log(row_total) - pick
    factor = jnp.exp(group_top - top) / row_total

    grads = []
    for i in range(NT // 2):
        pair = []
        for j in (2 * i, 2 * i + 1):
            hit = (row + j * 128 == target).astype(jnp.float32)
            pair.append((exponents[j] * factor - hit).astype(jnp.bfloat16))
        grads.append(jnp.concatenate(pair, axis=0))
    for k, e in OTHERS:
        if (k, e) != (2, 1):
            landed(wx.at[t_at(-k, e)], w_message[k, e])
    landed(wx.at[t_at(-2, 1), early], early_message)
    landed(wx.at[t_at(-2, 1), late], w_message[2, 1])

    def contribute(slots):
        part = None
        for i in range(NT // 2):
            rows = [
                jnp.concatenate([wx[2 * i, z_at(OFFSETS[slot])],
                                 wx[2 * i + 1, z_at(OFFSETS[slot])]], axis=1)
                for slot in slots
            ]
            term = jnp.dot(jnp.concatenate(rows, axis=0), grads[i],
                           preferred_element_type=jnp.float32)
            part = term if part is None else part + term
        for n, slot in enumerate(slots):
            pieces[slot] = part[64 * n:64 * (n + 1)]

    sum_halves = (pl.ds(0, 32), pl.ds(32, 32))
    far_pair_message = [new() for _ in NEAR]
    near_message = [new() for _ in NEAR]
    skip_message = [new(), new()]
    for i in (2, 3):
        contribute((7 + 2 * i, 8 + 2 * i))
        push(pieces.at[pl.ds(7 + 2 * i, 2)], near_far.at[i], far_pair_message[i], at_z(NEAR[i]))
    contribute((15,))
    for i, offset in ((0, 3), (1, -3)):
        push(pieces.at[15, sum_halves[i]], skip.at[i], skip_message[i], at_z(offset))
    for i in (0, 1):
        contribute((7 + 2 * i, 8 + 2 * i))
        push(pieces.at[pl.ds(7 + 2 * i, 2)], near_far.at[i], far_pair_message[i], at_z(NEAR[i]))
    contribute((3, 4, 1, 2))
    for i in (2, 3, 0, 1):
        push(pieces.at[1 + i], near_own.at[i], near_message[i], at_z(NEAR[i]))
    contribute((5, 6, 0))

    own_hit = (row + t * 128 == target).astype(jnp.float32)
    own_grad = (exponents[t] * factor - own_hit).astype(jnp.bfloat16)

    def weight_gradient(slots):
        for slot in slots:
            columns = pl.ds(pl.multiple_of(z_at(OFFSETS[slot]) * 512, 512), 512)
            d_weight_ref[:, columns] = lax.dot_general(
                own_grad, block(slot), (((1,), (1,)), ((), ())),
                preferred_element_type=jnp.float32).astype(jnp.bfloat16)

    weight_gradient(range(10))
    for i in range(4):
        landed(near_far.at[i], far_pair_message[i])
    for i in range(2):
        landed(skip.at[i], skip_message[i])
    far_message = [new(), new()]
    for i in (0, 1):
        pieces[5 + i] = (pieces[5 + i] + near_far[0, i] + near_far[1, i]
                         + near_far[2, i] + near_far[3, i])
        pieces[5 + i, sum_halves[i]] += skip[i]
        push(pieces.at[5 + i], far_sum.at[i], far_message[i], at_z(OFFSETS[5 + i]))
    weight_gradient(range(10, NZ))
    for i in range(4):
        landed(near_own.at[i], near_message[i])
    landed(far_sum.at[0], far_message[0])
    landed(far_sum.at[1], far_message[1])
    d_hidden_ref[...] = (pieces[0] + near_own[0] + near_own[1] + near_own[2] + near_own[3]
                         + far_sum[0] + far_sum[1]).astype(jnp.bfloat16)
    for _, copy in sent:
        copy.wait_send()
    assert count[0] <= MESSAGES


def deliver(a_ref, b_ref, c_ref, a_out, b_out, c_out, sem):
    copies = [
        pltpu.make_async_copy(b_ref, b_out, sem.at[0]),
        pltpu.make_async_copy(a_ref, a_out, sem.at[1]),
        pltpu.make_async_copy(c_ref, c_out, sem.at[2]),
    ]
    for copy in copies:
        copy.start()
    for copy in copies:
        copy.wait()


def on_device(hidden, weight, targets):
    vmem = pl.BlockSpec(memory_space=pltpu.VMEM)
    hbm = pl.BlockSpec(memory_space=pltpu.HBM)
    bf16, f32 = jnp.bfloat16, jnp.float32
    d_hidden, d_weight, losses = pl.pallas_call(
        kernel,
        out_shape=(
            jax.ShapeDtypeStruct((64, 128), bf16),
            jax.ShapeDtypeStruct((128, 8192), bf16),
            jax.ShapeDtypeStruct((1, 128), f32),
        ),
        in_specs=[hbm, hbm, hbm],
        out_specs=(vmem, vmem, vmem),
        scratch_shapes=[
            pltpu.VMEM((1, 128), jnp.int32),
            pltpu.VMEM((128, 8192), bf16),
            pltpu.VMEM((8, 16, 64, 128), bf16),
            pltpu.VMEM((8, 16, 64, 128), bf16),
            pltpu.VMEM((16, 8, 32, 128), bf16),
            pltpu.VMEM((16, 2, 4, 32, 128), bf16),
            pltpu.VMEM((8, 128, 128), f32),
            pltpu.VMEM((8, 128, 128), f32),
            pltpu.VMEM((8, 1, 384), f32),
            pltpu.VMEM((16, 1, 384), f32),
            pltpu.VMEM((1, 384), f32),
            pltpu.VMEM((1, 384), f32),
            pltpu.VMEM((16, 64, 128), f32),
            pltpu.VMEM((4, 64, 128), f32),
            pltpu.VMEM((4, 2, 64, 128), f32),
            pltpu.VMEM((2, 32, 128), f32),
            pltpu.VMEM((2, 64, 128), f32),
            pltpu.SemaphoreType.DMA((4,)),
            pltpu.SemaphoreType.DMA((MESSAGES,)),
            pltpu.SemaphoreType.DMA((MESSAGES,)),
        ],
        compiler_params=pltpu.CompilerParams(
            collective_id=0, has_side_effects=True, vmem_limit_bytes=50 * 2**20),
        cost_estimate=pl.CostEstimate(
            flops=3 * 2 * 128 * 128 * 8192, bytes_accessed=2 * 2 * 128 * 8192, transcendentals=0),
    )(hidden.T, weight, targets.reshape(1, 128))
    d_hidden, d_weight, losses = pl.pallas_call(
        deliver,
        out_shape=(
            jax.ShapeDtypeStruct((64, 128), bf16),
            jax.ShapeDtypeStruct((128, 8192), bf16),
            jax.ShapeDtypeStruct((1, 128), f32),
        ),
        in_specs=[pl.BlockSpec(memory_space=pl.ANY)] * 3,
        out_specs=[pl.BlockSpec(memory_space=pl.ANY)] * 3,
        scratch_shapes=[pltpu.SemaphoreType.DMA((3,))],
        compiler_params=pltpu.CompilerParams(vmem_limit_bytes=8 * 2**20),
        cost_estimate=pl.CostEstimate(
            flops=0, bytes_accessed=2 * 2 * 128 * 8192, transcendentals=0),
    )(d_hidden, d_weight, losses)
    return d_hidden.T, d_weight, losses.reshape(128)


def solution(mesh):
    in_specs = (P("dp", ("pipe", "tensor")), P(("dp", "pipe", "tensor"), None), P("dp"))
    out_specs = (P("dp", ("pipe", "tensor")), P(("dp", "pipe", "tensor"), None), P("dp"))
    return jax.shard_map(
        on_device, mesh=mesh, in_specs=in_specs, out_specs=out_specs, check_vma=False
    )
```
